32 devices in a mesh: ctx: 8 (over z, x), grp: 4 (over y, core).
Axes of the slice: x: 2, y: 2, z: 4, core: 2. Of those that a mesh axis runs over, the one named last changes fastest.
Arguments:
- queries: bfloat16 [32768, 512], P(('grp', 'ctx')), parts along dimension 0, may hold values from -6 to 6
- key_vectors: bfloat16 [32768, 512], P(('grp', 'ctx')), parts along dimension 0, may hold values from -6 to 6
- value_rows: bfloat16 [32768, 512], P(('grp', 'ctx')), parts along dimension 0, may hold values from -6 to 6
- cotangent: bfloat16 [32768, 512], P(('grp', 'ctx')), parts along dimension 0, may hold values from -6 to 6
Outputs:
- attended: bfloat16 [32768, 512], P(('grp', 'ctx')), parts along dimension 0
- grad_queries: bfloat16 [32768, 512], P(('grp', 'ctx')), parts along dimension 0
- grad_keys: bfloat16 [32768, 512], P(('grp', 'ctx')), parts along dimension 0
- grad_values: bfloat16 [32768, 512], P(('grp', 'ctx')), parts along dimension 0
The draws below stay inside these ranges and needn't reach their ends.
There are 4 independent parts, one for each index of `grp`. The reference program is written for one: setup_inputs(seed, part) draws one part's arguments, and reference() takes and returns one part's arrays. A program takes and returns all parts, laid end to end along the dimension named above; each array names one. Nothing has to cross between parts.
All inputs are finite; a program needn't handle non-finite values.
Results may differ from the reference program's by a relative error of at most 0.0025.
Values sent between devices are 32-bit elements; how exact they have to be, the bound alone decides.
No kernel may reach another device: no remote copies, remote signals or barrier semaphores. Data moves between devices by JAX's collectives and lax.ppermute only.
A program may use at most 128 MiB of HBM per device.

```python
import math
import jax
import jax.numpy as jnp
from jax import lax

DH = 128
HEADS = 4
L_DEV = 1024
SEQ = 8192
COLS = 512


def steps_of(rng, extent, shards, low, largest):
    gain, own = 1.0, jax.random.fold_in(rng, 6)
    for axis_at, blocks in shards:
        draws = jnp.exp(jax.random.uniform(jax.random.fold_in(own, axis_at), (blocks,), jnp.float32, low / len(shards), largest / len(shards)))
        gain = gain * jnp.repeat(draws, extent[axis_at] // blocks).reshape([-1 if axis == axis_at else 1 for axis in range(len(extent))])
    return gain


def gaussian(own_key, shape, scale, bound, shards=(), kind=jnp.bfloat16):
    level = steps_of(own_key, shape, shards, -0.22, 0.18) if shards else 1.0
    values = jax.random.normal(own_key, shape, jnp.float32) * scale * level
    return jnp.minimum(jnp.maximum(values, -bound), bound).astype(kind)


def setup_inputs(seed: int = 0, part: int = 0) -> dict:
    arg_keys = jax.random.split(jax.random.key(seed), 5)
    own_keys = jax.random.split(jax.random.fold_in(arg_keys[4], part), 5)
    queries = gaussian(own_keys[0], (SEQ, COLS), 1.0, 6.0, ((0, 8),))
    key_vectors = gaussian(own_keys[1], (SEQ, COLS), 1.0, 6.0, ((0, 8),))
    value_rows = gaussian(own_keys[2], (SEQ, COLS), 1.0, 6.0, ((0, 8),))
    cotangent = gaussian(own_keys[3], (SEQ, COLS), 1.0, 6.0, ((0, 8),))
    return dict(queries=queries, key_vectors=key_vectors, value_rows=value_rows, cotangent=cotangent)


def inner_first(left, right):
    return lax.dot_general(left, right, (((0,), (0,)), ((), ())), preferred_element_type=jnp.float32)

def inner_last(left, right):
    return lax.dot_general(left, right, (((1,), (1,)), ((), ())), preferred_element_type=jnp.float32)

def split_state(state):
    upper = lax.optimization_barrier(state.astype(jnp.bfloat16))
    lower = (state - upper.astype(jnp.float32)).astype(jnp.bfloat16)
    return (upper, lower)

def block_states(blocks):
    queries, key_vectors, value_rows, cotangent = blocks
    width = DH
    states = []
    grads = []
    for head_index in range(HEADS):
        cols = slice(head_index * width, (head_index + 1) * width)
        states.append(inner_first(key_vectors[:, cols], value_rows[:, cols]))
        grads.append(inner_first(queries[:, cols], cotangent[:, cols]))
    return (jnp.stack(states), jnp.stack(grads))

def block_outputs(queries, key_vectors, value_rows, cotangent, prefix_state, suffix_grad, factor):
    width = DH
    length = queries.shape[0]
    causal = lax.broadcasted_iota(jnp.int32, (length, length), 0) >= lax.broadcasted_iota(jnp.int32, (length, length), 1)
    results = ([], [], [], [])
    prefix_hi, prefix_lo = split_state(prefix_state)
    suffix_hi, suffix_lo = split_state(suffix_grad)
    for head_index in range(HEADS):
        cols = slice(head_index * width, (head_index + 1) * width)
        query_head = queries[:, cols]
        key_head = key_vectors[:, cols]
        value_head = value_rows[:, cols]
        cot_head = cotangent[:, cols]
        state_hi = prefix_hi[head_index]
        state_lo = prefix_lo[head_index]
        grad_hi = suffix_hi[head_index]
        grad_lo = suffix_lo[head_index]
        weights = jnp.where(causal, inner_last(query_head, key_head), 0.0).astype(jnp.bfloat16)
        back_weights = jnp.where(causal, inner_last(cot_head, value_head), 0.0).astype(jnp.bfloat16)
        attended = jnp.dot(weights, value_head, preferred_element_type=jnp.float32) + jnp.dot(query_head, state_hi, preferred_element_type=jnp.float32) + jnp.dot(query_head, state_lo, preferred_element_type=jnp.float32)
        grad_q = jnp.dot(back_weights, key_head, preferred_element_type=jnp.float32) + inner_last(cot_head, state_hi) + inner_last(cot_head, state_lo)
        grad_k = inner_first(back_weights, query_head) + inner_last(value_head, grad_hi) + inner_last(value_head, grad_lo)
        grad_v = inner_first(weights, cot_head) + jnp.dot(key_head, grad_hi, preferred_element_type=jnp.float32) + jnp.dot(key_head, grad_lo, preferred_element_type=jnp.float32)
        for target, source in zip(results, (attended, grad_q, grad_k, grad_v)):
            target.append((factor * source).astype(jnp.bfloat16))
    return tuple((jnp.concatenate(parts, axis=1) for parts in results))

def adding(running, increment):
    return (running + increment, running)

def reference(queries, key_vectors, value_rows, cotangent):
    factor = 1.0 / math.sqrt(DH * SEQ)
    nblocks = SEQ // L_DEV
    blocks = tuple((arr.reshape(nblocks, L_DEV, HEADS * DH) for arr in (queries, key_vectors, value_rows, cotangent)))
    states, grads = lax.map(block_states, blocks)
    zeros_state = jnp.zeros((HEADS, DH, DH), jnp.float32)
    _, prefix = lax.scan(adding, zeros_state, states)
    _, suffix = lax.scan(adding, zeros_state, grads, reverse=True)

    def per_block(packed):
        return block_outputs(packed[0][0], packed[0][1], packed[0][2], packed[0][3], packed[1], packed[2], factor)
    outputs = lax.map(per_block, (blocks, prefix, suffix))
    return tuple((result.reshape(SEQ, HEADS * DH) for result in outputs))
```

```python
import functools
import math

import jax
import jax.numpy as jnp
from jax import lax
from jax.experimental import pallas as pl
from jax.experimental.pallas import tpu as pltpu
from jax.sharding import PartitionSpec as P

DH = 128
HEADS = 4
CHUNK = 256
F32 = jnp.float32
BF16 = jnp.bfloat16


def mm(left, right):
    return lax.dot_general(left, right, (((1,), (0,)), ((), ())), preferred_element_type=F32)


def mm_first(left, right):
    return lax.dot_general(left, right, (((0,), (0,)), ((), ())), preferred_element_type=F32)


def mm_last(left, right):
    return lax.dot_general(left, right, (((1,), (1,)), ((), ())), preferred_element_type=F32)


def split(state):
    hi = state.astype(BF16)
    return hi, (state - hi.astype(F32)).astype(BF16)


def states_kernel(half_ref, q_ref, k_ref, v_ref, d_ref, out_ref):
    per = q_ref.shape[1] // DH
    for head in range(per):
        cols = slice(head * DH, (head + 1) * DH)
        out_ref[head] = mm_first(k_ref[:, cols], v_ref[:, cols])
        out_ref[per + head] = mm_first(q_ref[:, cols], d_ref[:, cols])


def half_states(half, queries, key_vectors, value_rows, cotangent):
    length, columns = queries.shape
    spec = pl.BlockSpec((length, columns // 2), lambda i, half_ref: (0, half_ref[0]))
    return pl.pallas_call(
        states_kernel,
        out_shape=jax.ShapeDtypeStruct((HEADS, DH, DH), F32),
        grid_spec=pltpu.PrefetchScalarGridSpec(
            num_scalar_prefetch=1,
            grid=(1,),
            in_specs=[spec] * 4,
            out_specs=pl.BlockSpec((HEADS, DH, DH), lambda i, half_ref: (0, 0, 0)),
        ),
        compiler_params=pltpu.CompilerParams(vmem_limit_bytes=40 * 2**20),
        cost_estimate=pl.CostEstimate(flops=2 * 2 * 2 * length * DH * DH, bytes_accessed=4 * length * columns, transcendentals=0),
        name="half_states",
    )(half, queries, key_vectors, value_rows, cotangent)


def final_kernel(factor, half_ref, q_ref, k_ref, v_ref, d_ref, pre_ref, suf_ref, *refs):
    att_ref, gq_ref, gk_ref, gv_ref = refs[-4:]
    length = q_ref.shape[0]
    chunks = length // CHUNK
    rows = lax.broadcasted_iota(jnp.int32, (CHUNK, CHUNK), 0)
    cols = lax.broadcasted_iota(jnp.int32, (CHUNK, CHUNK), 1)
    lower = rows >= cols
    upper = rows <= cols
    state = pre_ref[0]
    for c in range(chunks):
        at = slice(c * CHUNK, (c + 1) * CHUNK)
        q, k, v, d = q_ref[at, :], k_ref[at, :], v_ref[at, :], d_ref[at, :]
        hi, lo = split(state)
        weights = jnp.where(lower, mm_last(q, k), 0.0).astype(BF16)
        back = jnp.where(lower, mm_last(d, v), 0.0).astype(BF16)
        att = mm(weights, v) + mm(jnp.concatenate([q, q], 1), jnp.concatenate([hi, lo], 0))
        gq = mm(back, k) + mm_last(jnp.concatenate([d, d], 1), jnp.concatenate([hi, lo], 1))
        att_ref[at, :] = (factor * att).astype(BF16)
        gq_ref[at, :] = (factor * gq).astype(BF16)
        if c < chunks - 1:
            state = state + mm_first(k, v)
    state = suf_ref[0]
    for c in reversed(range(chunks)):
        at = slice(c * CHUNK, (c + 1) * CHUNK)
        q, k, v, d = q_ref[at, :], k_ref[at, :], v_ref[at, :], d_ref[at, :]
        hi, lo = split(state)
        weights = jnp.where(upper, mm_last(k, q), 0.0).astype(BF16)
        back = jnp.where(upper, mm_last(v, d), 0.0).astype(BF16)
        gk = mm(back, q) + mm_last(jnp.concatenate([v, v], 1), jnp.concatenate([hi, lo], 1))
        gv = mm(weights, d) + mm(jnp.concatenate([k, k], 1), jnp.concatenate([hi, lo], 0))
        gk_ref[at, :] = (factor * gk).astype(BF16)
        gv_ref[at, :] = (factor * gv).astype(BF16)
        if c > 0:
            state = state + mm_first(q, d)


def half_outputs(factor, half, arrays, prefix, suffix, previous=()):
    length, columns = arrays[0].shape
    per = HEADS // 2
    wide = pl.BlockSpec((length, DH), lambda i, half_ref: (0, half_ref[0] * per + i))
    state = pl.BlockSpec((1, DH, DH), lambda i, half_ref: (i, 0, 0))
    out = jax.ShapeDtypeStruct((length, columns), BF16)
    return pl.pallas_call(
        functools.partial(final_kernel, factor),
        out_shape=[out] * 4,
        grid_spec=pltpu.PrefetchScalarGridSpec(
            num_scalar_prefetch=1,
            grid=(per,),
            in_specs=[wide] * 4 + [state] * 2 + [pl.BlockSpec(memory_space=pl.ANY)] * len(previous),
            out_specs=[wide] * 4,
        ),
        input_output_aliases={7 + i: i for i in range(len(previous))},
        compiler_params=pltpu.CompilerParams(vmem_limit_bytes=40 * 2**20),
        cost_estimate=pl.CostEstimate(flops=per * 2 * 1024 * 128 * 128 * 16, bytes_accessed=8 * length * columns, transcendentals=0),
        name="half_outputs",
    )(half, *arrays, prefix, suffix, *previous)


def swap(value, bit, devices):
    return lax.ppermute(value, "ctx", [(i, i ^ bit) for i in range(devices)])


def on_device(queries, key_vectors, value_rows, cotangent):
    devices = lax.axis_size("ctx")
    length = queries.shape[0]
    factor = 1.0 / math.sqrt(DH * length * devices)
    per = HEADS // 2
    arrays = (queries, key_vectors, value_rows, cotangent)
    me = lax.axis_index("ctx")
    last = lax.rem(me, 2)
    own = jnp.reshape(last, (1,))
    other = 1 - own
    send = half_states(other, *arrays)
    got = swap(send, 1, devices)
    keep = half_states(own, *arrays)
    total = keep + got
    prefix = jnp.zeros((per, DH, DH), F32)
    suffix = prefix
    bit = 2
    while bit < devices:
        high = (me & bit) != 0
        if bit * 2 < devices:
            part = swap(total, bit, devices)
            total = total + part
            prefix = prefix + jnp.where(high, part[:per], 0.0)
            suffix = suffix + jnp.where(high, 0.0, part[per:])
        else:
            part = swap(jnp.where(high, total[per:], total[:per]), bit, devices)
            prefix = prefix + jnp.where(high, part, 0.0)
            suffix = suffix + jnp.where(high, 0.0, part)
        bit *= 2
    first = last == 0
    give_prefix = prefix + jnp.where(first, keep[:per], 0.0)
    give_suffix = suffix + jnp.where(first, 0.0, keep[per:])
    taken = swap(jnp.concatenate([give_prefix, give_suffix]), 1, devices)
    own_prefix = prefix + jnp.where(first, 0.0, got[:per])
    own_suffix = suffix + jnp.where(first, got[per:], 0.0)
    outs = half_outputs(factor, own, arrays, own_prefix, own_suffix)
    return tuple(half_outputs(factor, other, arrays, taken[:per], taken[per:], tuple(outs)))


def solution(mesh):
    spec = P(("grp", "ctx"), None)
    return jax.shard_map(
        on_device, mesh=mesh, in_specs=(spec,) * 4, out_specs=(spec,) * 4, check_vma=False
    )
```

```python
import functools
import math

import jax
import jax.numpy as jnp
from jax import lax
from jax.experimental import pallas as pl
from jax.experimental.pallas import tpu as pltpu
from jax.sharding import PartitionSpec as P

DH = 128
HEADS = 4
PER = HEADS // 2
CHUNK = 256
F32 = jnp.float32
BF16 = jnp.bfloat16
MIB = 2**20
VMEM = pl.BlockSpec(memory_space=pltpu.VMEM)
SMEM = pl.BlockSpec(memory_space=pltpu.SMEM)
HBM = pl.BlockSpec(memory_space=pltpu.HBM)


def mm(left, right):
    return lax.dot_general(left, right, (((1,), (0,)), ((), ())), preferred_element_type=F32)


def mm_first(left, right):
    return lax.dot_general(left, right, (((0,), (0,)), ((), ())), preferred_element_type=F32)


def mm_last(left, right):
    return lax.dot_general(left, right, (((1,), (1,)), ((), ())), preferred_element_type=F32)


def split(state):
    hi = state.astype(BF16)
    return hi, (state - hi.astype(F32)).astype(BF16)


def half_columns(half_ref):
    return pl.ds(pl.multiple_of(half_ref[0] * (PER * DH), PER * DH), PER * DH)


def states_kernel(half_ref, q_hbm, k_hbm, v_hbm, d_hbm, out_ref, q_ref, k_ref, v_ref, d_ref, sems):
    at = half_columns(half_ref)
    pairs = ((k_hbm, k_ref), (v_hbm, v_ref), (q_hbm, q_ref), (d_hbm, d_ref))
    copies = [
        pltpu.make_async_copy(source.at[:, at], target, sems.at[i])
        for i, (source, target) in enumerate(pairs)
    ]
    for copy in copies:
        copy.start()
    for pair, (left, right) in enumerate(((k_ref, v_ref), (q_ref, d_ref))):
        copies[2 * pair].wait()
        copies[2 * pair + 1].wait()
        for head in range(PER):
            cols = slice(head * DH, (head + 1) * DH)
            out_ref[pair * PER + head] = mm_first(left[:, cols], right[:, cols])


def half_states(half, arrays):
    length = arrays[0].shape[0]
    return pl.pallas_call(
        states_kernel,
        out_shape=jax.ShapeDtypeStruct((HEADS, DH, DH), F32),
        in_specs=[SMEM] + [HBM] * 4,
        out_specs=VMEM,
        scratch_shapes=[pltpu.VMEM((length, PER * DH), BF16)] * 4 + [pltpu.SemaphoreType.DMA((4,))],
        compiler_params=pltpu.CompilerParams(vmem_limit_bytes=16 * MIB),
        cost_estimate=pl.CostEstimate(flops=8 * length * DH * DH, bytes_accessed=8 * length * PER * DH, transcendentals=0),
        name="half_states",
    )(half, *arrays)


def local_kernel(half_ref, after_ref, q_ref, k_ref, v_ref, d_ref, att_ref, gq_ref, gk_ref, gv_ref, keep_ref):
    length = q_ref.shape[0]
    chunks = length // CHUNK
    rows = lax.broadcasted_iota(jnp.int32, (CHUNK, CHUNK), 0)
    cols = lax.broadcasted_iota(jnp.int32, (CHUNK, CHUNK), 1)
    lower = rows >= cols
    upper = rows <= cols
    for head in range(PER):
        columns = pl.ds(pl.multiple_of((half_ref[0] * PER + head) * DH, DH), DH)
        state = None
        for c in range(chunks):
            at = slice(c * CHUNK, (c + 1) * CHUNK)
            q, k, v, d = q_ref[at, columns], k_ref[at, columns], v_ref[at, columns], d_ref[at, columns]
            weights = jnp.where(lower, mm_last(q, k), 0.0).astype(BF16)
            back = jnp.where(lower, mm_last(d, v), 0.0).astype(BF16)
            att = mm(weights, v)
            gq = mm(back, k)
            if c:
                hi, lo = split(state)
                att += mm(jnp.concatenate([q, q], 1), jnp.concatenate([hi, lo], 0))
                gq += mm_last(jnp.concatenate([d, d], 1), jnp.concatenate([hi, lo], 1))
            att_ref[head, at, :] = att
            gq_ref[head, at, :] = gq
            new = mm_first(k, v)
            state = new if state is None else state + new
        keep_ref[head] = state
        state = None
        for c in reversed(range(chunks)):
            at = slice(c * CHUNK, (c + 1) * CHUNK)
            q, k, v, d = q_ref[at, columns], k_ref[at, columns], v_ref[at, columns], d_ref[at, columns]
            weights = jnp.where(upper, mm_last(k, q), 0.0).astype(BF16)
            back = jnp.where(upper, mm_last(v, d), 0.0).astype(BF16)
            gk = mm(back, q)
            gv = mm(weights, d)
            if c < chunks - 1:
                hi, lo = split(state)
                gk += mm_last(jnp.concatenate([v, v], 1), jnp.concatenate([hi, lo], 1))
                gv += mm(jnp.concatenate([k, k], 1), jnp.concatenate([hi, lo], 0))
            gk_ref[head, at, :] = gk
            gv_ref[head, at, :] = gv
            new = mm_first(q, d)
            state = new if state is None else state + new
        keep_ref[PER + head] = state


def local_products(half, arrays, after):
    length, columns = arrays[0].shape
    return pl.pallas_call(
        local_kernel,
        out_shape=[jax.ShapeDtypeStruct((PER, length, DH), F32)] * 4 + [jax.ShapeDtypeStruct((HEADS, DH, DH), F32)],
        in_specs=[SMEM] + [VMEM] * 5,
        out_specs=[VMEM] * 5,
        compiler_params=pltpu.CompilerParams(vmem_limit_bytes=16 * MIB),
        cost_estimate=pl.CostEstimate(
            flops=PER * 16 * length * CHUNK * DH, bytes_accessed=8 * length * columns, transcendentals=0
        ),
        name="local_products",
    )(half, after, *arrays)


def final_kernel(factor, half_ref, q_ref, k_ref, v_ref, d_ref, pre_ref, suf_ref, att_ref, gq_ref, gk_ref, gv_ref, *refs):
    outs, stage, sems = refs[-6:-2], refs[-2], refs[-1]
    copies = []
    for head in range(PER):
        columns = pl.ds(pl.multiple_of((half_ref[0] * PER + head) * DH, DH), DH)
        hi, lo = split(pre_ref[head])
        suf_hi, suf_lo = split(suf_ref[head])
        down = jnp.concatenate([hi, lo], 0)
        along = jnp.concatenate([hi, lo], 1)
        suf_down = jnp.concatenate([suf_hi, suf_lo], 0)
        suf_along = jnp.concatenate([suf_hi, suf_lo], 1)
        work = (
            (q_ref, down, mm, att_ref),
            (d_ref, along, mm_last, gq_ref),
            (v_ref, suf_along, mm_last, gk_ref),
            (k_ref, suf_down, mm, gv_ref),
        )
        for i, (source, state, product, local) in enumerate(work):
            rows = source[:, columns]
            value = product(jnp.concatenate([rows, rows], 1), state) + local[head]
            stage[i, head] = (factor * value).astype(BF16)
            copy = pltpu.make_async_copy(stage.at[i, head], outs[i].at[:, columns], sems.at[i, head])
            copy.start()
            copies.append(copy)
    for copy in copies:
        copy.wait()


def half_outputs(factor, half, arrays, prefix, suffix, local, previous=()):
    length, columns = arrays[0].shape
    out = jax.ShapeDtypeStruct((length, columns), BF16)
    return pl.pallas_call(
        functools.partial(final_kernel, factor),
        out_shape=[out] * 4,
        in_specs=[SMEM] + [VMEM] * 10 + [HBM] * len(previous),
        out_specs=[HBM] * 4,
        scratch_shapes=[pltpu.VMEM((4, PER, length, DH), BF16), pltpu.SemaphoreType.DMA((4, PER))],
        input_output_aliases={11 + i: i for i in range(len(previous))},
        compiler_params=pltpu.CompilerParams(vmem_limit_bytes=16 * MIB),
        cost_estimate=pl.CostEstimate(
            flops=PER * 16 * length * DH * DH, bytes_accessed=8 * length * columns, transcendentals=0
        ),
        name="half_outputs",
    )(half, *arrays, prefix, suffix, *local, *previous)


def add_kernel(left_ref, right_ref, out_ref):
    out_ref[...] = left_ref[...] + right_ref[...]


SMALL = pltpu.CompilerParams(vmem_limit_bytes=4 * MIB)


def add_states(left, right):
    return pl.pallas_call(
        add_kernel,
        out_shape=jax.ShapeDtypeStruct(left.shape, F32),
        in_specs=[VMEM] * 2,
        out_specs=VMEM,
        compiler_params=SMALL,
        name="add_states",
    )(left, right)


def part_kernel(high_ref, left_ref, right_ref, after_ref, out_ref):
    at = pl.ds(high_ref[0] * PER, PER)
    out_ref[...] = left_ref[at] + right_ref[at]


def add_part(high, left, right, after):
    return pl.pallas_call(
        part_kernel,
        out_shape=jax.ShapeDtypeStruct((PER, DH, DH), F32),
        in_specs=[SMEM] + [VMEM] * 3,
        out_specs=VMEM,
        compiler_params=SMALL,
        name="add_part",
    )(high, left, right, after)


def join_kernel(bits, me_ref, after_ref, keep_ref, got_ref, last_ref, *refs):
    parts, (give_ref, pre_ref, suf_ref) = refs[:-3], refs[-3:]
    me = me_ref[0]
    high = [(lax.rem(lax.div(me, bit), 2) == 1) for bit in bits]
    first = lax.rem(me, 2) == 0
    last = last_ref[...]
    zero = jnp.zeros_like(last)
    prefix = jnp.where(high[-1], last, zero)
    suffix = jnp.where(high[-1], zero, last)
    for up, part_ref in zip(high, parts):
        prefix += jnp.where(up, part_ref[:PER], zero)
        suffix += jnp.where(up, zero, part_ref[PER:])
    give_ref[:PER] = prefix + jnp.where(first, keep_ref[:PER], zero)
    give_ref[PER:] = suffix + jnp.where(first, zero, keep_ref[PER:])
    pre_ref[...] = prefix + jnp.where(first, zero, got_ref[:PER])
    suf_ref[...] = suffix + jnp.where(first, got_ref[PER:], zero)


def join(bits, me, after, keep, got, last, parts):
    half = jax.ShapeDtypeStruct((PER, DH, DH), F32)
    return pl.pallas_call(
        functools.partial(join_kernel, bits),
        out_shape=[jax.ShapeDtypeStruct((HEADS, DH, DH), F32), half, half],
        in_specs=[SMEM] + [VMEM] * (4 + len(parts)),
        out_specs=[VMEM] * 3,
        compiler_params=SMALL,
        name="join_states",
    )(me, after, keep, got, last, *parts)


def swap(value, bit, devices):
    return lax.ppermute(value, "ctx", [(i, i ^ bit) for i in range(devices)])


def on_device(queries, key_vectors, value_rows, cotangent):
    devices = lax.axis_size("ctx")
    length = queries.shape[0]
    factor = 1.0 / math.sqrt(DH * length * devices)
    arrays = (queries, key_vectors, value_rows, cotangent)
    held = tuple(pltpu.with_memory_space_constraint(array, pltpu.HBM) for array in arrays)
    me = jnp.reshape(lax.axis_index("ctx"), (1,))
    own = me & 1
    other = 1 - own
    send = half_states(other, held)
    got = swap(send, 1, devices)
    keep = half_states(own, held)
    total = add_states(keep, got)
    bits = []
    parts = []
    bit = 2
    while bit * 2 < devices:
        part = swap(total, bit, devices)
        bits.append(bit)
        parts.append(part)
        if bit * 4 < devices:
            total = add_states(total, part)
        bit *= 2
    *own_local, own_keep = local_products(own, arrays, total)
    bits.append(bit)
    sent = add_part((me // bit) & 1, total, parts[-1], own_keep)
    last = swap(sent, bit, devices)
    *other_local, other_keep = local_products(other, arrays, sent)
    give, prefix, suffix = join(tuple(bits), me, other_keep, keep, got, last, parts)
    taken = swap(give, 1, devices)
    outs = half_outputs(factor, own, arrays, prefix, suffix, own_local)
    return tuple(half_outputs(factor, other, arrays, taken[:PER], taken[PER:], other_local, tuple(outs)))


def solution(mesh):
    spec = P(("grp", "ctx"), None)
    return jax.shard_map(
        on_device, mesh=mesh, in_specs=(spec,) * 4, out_specs=(spec,) * 4, check_vma=False
    )
```

```python
import functools
import math

import jax
import jax.numpy as jnp
from jax import lax
from jax.experimental import pallas as pl
from jax.experimental.pallas import tpu as pltpu
from jax.sharding import PartitionSpec as P

DH = 128
HEADS = 4
QUAD = 4
EARLY = ()
ORDER = (1, 2, 3)
CHUNK = 256
F32 = jnp.float32
BF16 = jnp.bfloat16
MIB = 2**20
VMEM = pl.BlockSpec(memory_space=pltpu.VMEM)
SMEM = pl.BlockSpec(memory_space=pltpu.SMEM)
HBM = pl.BlockSpec(memory_space=pltpu.HBM)


def mm(left, right):
    return lax.dot_general(left, right, (((1,), (0,)), ((), ())), preferred_element_type=F32)


def mm_first(left, right):
    return lax.dot_general(left, right, (((0,), (0,)), ((), ())), preferred_element_type=F32)


def mm_last(left, right):
    return lax.dot_general(left, right, (((1,), (1,)), ((), ())), preferred_element_type=F32)


def split(state):
    hi = state.astype(BF16)
    return hi, (state - hi.astype(F32)).astype(BF16)


def head_columns(me_ref, k):
    return pl.ds(pl.multiple_of((lax.rem(me_ref[0], QUAD) ^ k) * DH, DH), DH)


def params(mib):
    return pltpu.CompilerParams(vmem_limit_bytes=mib * MIB)


def states_kernel(ks, me_ref, q_hbm, k_hbm, v_hbm, d_hbm, *refs):
    outs, (q_ref, k_ref, v_ref, d_ref, sems) = refs[: len(ks)], refs[len(ks) :]
    pairs = ((k_hbm, k_ref), (v_hbm, v_ref), (q_hbm, q_ref), (d_hbm, d_ref))
    copies = [
        [
            pltpu.make_async_copy(source.at[:, head_columns(me_ref, k)], target.at[n], sems.at[n, i])
            for i, (source, target) in enumerate(pairs)
        ]
        for n, k in enumerate(ks)
    ]
    for group in copies:
        for copy in group:
            copy.start()
    for n in range(len(ks)):
        for copy in copies[n][:2]:
            copy.wait()
        outs[n][0] = mm_first(k_ref[n], v_ref[n])
        for copy in copies[n][2:]:
            copy.wait()
        outs[n][1] = mm_first(q_ref[n], d_ref[n])


def head_states(ks, me, arrays):
    length = arrays[0].shape[0]
    return pl.pallas_call(
        functools.partial(states_kernel, ks),
        out_shape=[jax.ShapeDtypeStruct((2, DH, DH), F32)] * len(ks),
        in_specs=[SMEM] + [HBM] * 4,
        out_specs=[VMEM] * len(ks),
        scratch_shapes=[pltpu.VMEM((len(ks), length, DH), BF16)] * 4 + [pltpu.SemaphoreType.DMA((len(ks), 4))],
        compiler_params=params(16),
        cost_estimate=pl.CostEstimate(
            flops=4 * len(ks) * length * DH * DH, bytes_accessed=8 * len(ks) * length * DH, transcendentals=0
        ),
        name="head_states",
    )(me, *arrays)


def local_kernel(which, me_ref, after_ref, q_ref, k_ref, v_ref, d_ref, att_ref, gq_ref, gk_ref, gv_ref, sub_ref, keep_ref):
    chunks = q_ref.shape[0] // CHUNK
    rows = lax.broadcasted_iota(jnp.int32, (CHUNK, CHUNK), 0)
    cols = lax.broadcasted_iota(jnp.int32, (CHUNK, CHUNK), 1)
    lower = rows >= cols
    upper = rows <= cols
    columns = head_columns(me_ref, which)
    state = jnp.zeros((DH, DH), F32)
    grads = []
    for c in range(chunks):
        at = slice(c * CHUNK, (c + 1) * CHUNK)
        q, k, v, d = q_ref[at, columns], k_ref[at, columns], v_ref[at, columns], d_ref[at, columns]
        weights = jnp.where(lower, mm_last(q, k), 0.0).astype(BF16)
        back = jnp.where(lower, mm_last(d, v), 0.0).astype(BF16)
        weights_t = jnp.where(upper, mm_last(k, q), 0.0).astype(BF16)
        back_t = jnp.where(upper, mm_last(v, d), 0.0).astype(BF16)
        att_ref[at, :] = mm(weights, v)
        gq_ref[at, :] = mm(back, k)
        gk_ref[at, :] = mm(back_t, q)
        gv_ref[at, :] = mm(weights_t, d)
        sub_ref[c, 0] = state
        state = state + mm_first(k, v)
        grads.append(mm_first(q, d))
    keep_ref[0] = state
    state = jnp.zeros((DH, DH), F32)
    for c in reversed(range(chunks)):
        sub_ref[c, 1] = state
        state = state + grads[c]
    keep_ref[1] = state


def local_products(which, me, arrays, after):
    length = arrays[0].shape[0]
    chunks = length // CHUNK
    *products, keep = pl.pallas_call(
        functools.partial(local_kernel, which),
        out_shape=[jax.ShapeDtypeStruct((length, DH), F32)] * 4
        + [jax.ShapeDtypeStruct((chunks, 2, DH, DH), F32), jax.ShapeDtypeStruct((2, DH, DH), F32)],
        in_specs=[SMEM] + [VMEM] * 5,
        out_specs=[VMEM] * 6,
        compiler_params=params(16),
        cost_estimate=pl.CostEstimate(
            flops=16 * length * CHUNK * DH, bytes_accessed=8 * length * DH, transcendentals=0
        ),
        name="local_products",
    )(me, after, *arrays)
    return products, keep


def final_kernel(factor, which, count, earlier, last, me_ref, q_ref, k_ref, v_ref, d_ref, *refs):
    given, refs = refs[:count], refs[count:]
    (att_ref, gq_ref, gk_ref, gv_ref, sub_ref), refs = refs[:5], refs[5:]
    staged, refs = refs[: len(earlier)], refs[len(earlier) :]
    columns = head_columns(me_ref, which)
    copies = []
    if last is None:
        (stage,) = refs
    else:
        *outs, stage, sems = refs[-6:]
    for row, (k, source) in enumerate(zip(earlier, staged)):
        for i in range(4):
            copies.append(pltpu.make_async_copy(source.at[i], outs[i].at[:, head_columns(me_ref, k)], sems.at[row, i]))
    for copy in copies:
        copy.start()
    chunks = q_ref.shape[0] // CHUNK
    prefix, suffix = given[0][0], given[0][1]
    if count == 2 and given[1].shape[0] == 1:
        high = lax.rem(lax.div(me_ref[0], QUAD), 2) == 1
        zero = jnp.zeros((DH, DH), F32)
        prefix += jnp.where(high, given[1][0], zero)
        suffix += jnp.where(high, zero, given[1][0])
    elif count == 2:
        prefix += given[1][0]
        suffix += given[1][1]
    states = [split(prefix + sub_ref[c, 0]) for c in range(chunks)]
    grads = [split(suffix + sub_ref[c, 1]) for c in range(chunks)]
    work = (
        (q_ref, states, mm, att_ref),
        (d_ref, states, mm_last, gq_ref),
        (v_ref, grads, mm_last, gk_ref),
        (k_ref, grads, mm, gv_ref),
    )
    for i, (source, parts, product, local) in enumerate(work):
        for c, (hi, lo) in enumerate(parts):
            at = slice(c * CHUNK, (c + 1) * CHUNK)
            rows = source[at, columns]
            value = local[at, :] + product(rows, hi) + product(rows, lo)
            stage[i, at, :] = (factor * value).astype(BF16)
        if last is not None:
            copy = pltpu.make_async_copy(stage.at[i], outs[i].at[:, columns], sems.at[len(earlier), i])
            copy.start()
            copies.append(copy)
    for copy in copies:
        copy.wait()


def head_outputs(factor, which, me, arrays, given, local, staged=(), outs=None):
    length, columns = arrays[0].shape
    staging = (4, length, DH)
    earlier = tuple(k for k, _ in staged)
    inputs = [me, *arrays, *given, *local, *(value for _, value in staged)]
    in_specs = [SMEM] + [VMEM] * (len(inputs) - 1)
    if outs is None:
        out_shape, out_specs = [jax.ShapeDtypeStruct(staging, BF16)], [VMEM]
        scratch, aliases = [], {}
    else:
        out_shape, out_specs = [jax.ShapeDtypeStruct((length, columns), BF16)] * 4, [HBM] * 4
        scratch = [pltpu.VMEM(staging, BF16), pltpu.SemaphoreType.DMA((len(earlier) + 1, 4))]
        aliases = {len(inputs) + i: i for i in range(len(outs))}
        in_specs += [HBM] * len(outs)
    return pl.pallas_call(
        functools.partial(final_kernel, factor, which, len(given), earlier, None if outs is None else bool(outs)),
        out_shape=out_shape,
        in_specs=in_specs,
        out_specs=out_specs,
        scratch_shapes=scratch,
        input_output_aliases=aliases,
        compiler_params=params(16),
        cost_estimate=pl.CostEstimate(
            flops=16 * length * DH * DH, bytes_accessed=8 * length * DH, transcendentals=0
        ),
        name="head_outputs",
    )(*inputs, *(outs or ()))


def total_kernel(me_ref, after_ref, *refs):
    pieces, out_ref = refs[:-1], refs[-1]
    total = pieces[0][...]
    for piece in pieces[1:]:
        total += piece[...]
    out_ref[...] = total


def part_kernel(bit, me_ref, after_ref, *refs):
    pieces, out_ref = refs[:-1], refs[-1]
    at = pl.ds(lax.rem(lax.div(me_ref[0], bit), 2), 1)
    total = pieces[0][at]
    for piece in pieces[1:]:
        total += piece[at]
    out_ref[...] = total


def combine(kernel, states, me, after, pieces, name):
    return pl.pallas_call(
        kernel,
        out_shape=jax.ShapeDtypeStruct((states, DH, DH), F32),
        in_specs=[SMEM] + [VMEM] * (1 + len(pieces)),
        out_specs=VMEM,
        compiler_params=params(4),
        name=name,
    )(me, after, *pieces)


def parts_kernel(me_ref, after_ref, *refs):
    pieces, outs = refs[:QUAD], refs[QUAD:]
    rank = lax.rem(me_ref[0], QUAD)
    zero = jnp.zeros((DH, DH), F32)
    for k, out in enumerate(outs):
        prefix, suffix = zero, zero
        for j, piece in enumerate(pieces):
            if j != k:
                before = (rank ^ j) < (rank ^ k)
                prefix += jnp.where(before, piece[0], zero)
                suffix += jnp.where(before, zero, piece[1])
        out[0] = prefix
        out[1] = suffix


def quad_parts(me, after, pieces):
    return pl.pallas_call(
        parts_kernel,
        out_shape=[jax.ShapeDtypeStruct((2, DH, DH), F32)] * QUAD,
        in_specs=[SMEM] + [VMEM] * (1 + QUAD),
        out_specs=[VMEM] * QUAD,
        compiler_params=params(4),
        name="quad_parts",
    )(me, after, *pieces)


def base_kernel(bits, me_ref, last_ref, *refs):
    parts, out_ref = refs[:-1], refs[-1]
    high = [lax.rem(lax.div(me_ref[0], bit), 2) == 1 for bit in bits]
    zero = jnp.zeros((DH, DH), F32)
    prefix = jnp.where(high[-1], last_ref[0], zero)
    suffix = jnp.where(high[-1], zero, last_ref[0])
    for up, part in zip(high, parts):
        prefix += jnp.where(up, part[0], zero)
        suffix += jnp.where(up, zero, part[1])
    out_ref[0] = prefix
    out_ref[1] = suffix


def quad_base(bits, me, last, parts):
    return pl.pallas_call(
        functools.partial(base_kernel, bits),
        out_shape=jax.ShapeDtypeStruct((2, DH, DH), F32),
        in_specs=[SMEM] + [VMEM] * (1 + len(parts)),
        out_specs=VMEM,
        compiler_params=params(4),
        name="quad_base",
    )(me, last, *parts)


def whole_kernel(me_ref, after_ref, base_ref, *refs):
    half = len(refs) // 2
    for part_ref, out_ref in zip(refs[:half], refs[half:]):
        if base_ref.shape[0] == 1:
            high = lax.rem(lax.div(me_ref[0], QUAD), 2) == 1
            zero = jnp.zeros((DH, DH), F32)
            out_ref[0] = part_ref[0] + jnp.where(high, base_ref[0], zero)
            out_ref[1] = part_ref[1] + jnp.where(high, zero, base_ref[0])
        else:
            out_ref[...] = part_ref[...] + base_ref[...]


def whole_states(me, after, base, parts):
    return pl.pallas_call(
        whole_kernel,
        out_shape=[jax.ShapeDtypeStruct((2, DH, DH), F32)] * len(parts),
        in_specs=[SMEM] + [VMEM] * (2 + len(parts)),
        out_specs=[VMEM] * len(parts),
        compiler_params=params(4),
        name="whole_states",
    )(me, after, base, *parts)


def swap(value, bit):
    return lax.ppermute(value, "ctx", [(i, i ^ bit) for i in range(lax.axis_size("ctx"))])


def on_device(queries, key_vectors, value_rows, cotangent):
    devices = lax.axis_size("ctx")
    factor = 1.0 / math.sqrt(DH * queries.shape[0] * devices)
    arrays = (queries, key_vectors, value_rows, cotangent)
    held = tuple(pltpu.with_memory_space_constraint(array, pltpu.HBM) for array in arrays)
    me = jnp.reshape(lax.axis_index("ctx"), (1,))
    local = [None] * QUAD
    send1, send2 = head_states((1, 2), me, held)
    got1 = swap(send1, 1)
    got2 = swap(send2, 2)
    (send3,) = head_states((3,), me, held)
    got3 = swap(send3, 3)
    local[0], keep = local_products(0, me, arrays, send3)
    local[1], after = local_products(1, me, arrays, keep)
    local[2], after = local_products(2, me, arrays, after)
    pieces = (keep, got1, got2, got3)
    known = pieces
    bits = []
    parts = []
    bit = QUAD
    while bit * 2 < devices:
        total = combine(total_kernel, 2, me, after, known, "sum_states")
        part = swap(total, bit)
        bits.append(bit)
        parts.append(part)
        known = (total, part)
        bit *= 2
    bits.append(bit)
    chosen = combine(functools.partial(part_kernel, bit), 1, me, after, known, "pick_state")
    base = swap(chosen, bit)
    mine = quad_parts(me, chosen, pieces)
    early = {k: swap(mine[k], k) for k in EARLY}
    local[3], after = local_products(3, me, arrays, mine[0])
    if parts:
        base = quad_base(tuple(bits), me, base, parts)
    late = [k for k in range(1, QUAD) if k not in EARLY]
    given = {0: (mine[0], base)}
    if late:
        for k, whole in zip(late, whole_states(me, after, base, [mine[k] for k in late])):
            given[k] = (swap(whole, k),)
    for k in EARLY:
        given[k] = (early[k], swap(base, k))
    outs = head_outputs(factor, 0, me, arrays, given[0], local[0], outs=())
    staged = [(k, head_outputs(factor, k, me, arrays, given[k], local[k])[0]) for k in ORDER[:2]]
    k = ORDER[2]
    return tuple(head_outputs(factor, k, me, arrays, given[k], local[k], staged, outs))


def solution(mesh):
    spec = P(("grp", "ctx"), None)
    return jax.shard_map(
        on_device, mesh=mesh, in_specs=(spec,) * 4, out_specs=(spec,) * 4, check_vma=False
    )
```

```python
import functools
import math

import jax
import jax.numpy as jnp
from jax import lax
from jax.experimental import pallas as pl
from jax.experimental.pallas import tpu as pltpu
from jax.sharding import PartitionSpec as P

DH = 128
HEADS = 4
QUAD = 4
EARLY = ()
ORDER = (3, 1, 2)
CHUNK = 256
F32 = jnp.float32
BF16 = jnp.bfloat16
MIB = 2**20
VMEM = pl.BlockSpec(memory_space=pltpu.VMEM)
SMEM = pl.BlockSpec(memory_space=pltpu.SMEM)
HBM = pl.BlockSpec(memory_space=pltpu.HBM)


def mm(left, right):
    return lax.dot_general(left, right, (((1,), (0,)), ((), ())), preferred_element_type=F32)


def mm_first(left, right):
    return lax.dot_general(left, right, (((0,), (0,)), ((), ())), preferred_element_type=F32)


def mm_last(left, right):
    return lax.dot_general(left, right, (((1,), (1,)), ((), ())), preferred_element_type=F32)


def split(state):
    hi = state.astype(BF16)
    return hi, (state - hi.astype(F32)).astype(BF16)


def head_columns(me_ref, k):
    return pl.ds(pl.multiple_of((lax.rem(me_ref[0], QUAD) ^ k) * DH, DH), DH)


def params(mib):
    return pltpu.CompilerParams(vmem_limit_bytes=mib * MIB)


def sub_states(left, right, axis, sub_ref, total_ref):
    chunks = left.shape[0] // CHUNK
    state = jnp.zeros((DH, DH), F32)
    for c in range(chunks) if axis == 0 else reversed(range(chunks)):
        at = slice(c * CHUNK, (c + 1) * CHUNK)
        sub_ref[c, axis] = state
        state = state + mm_first(left[at], right[at])
    total_ref[axis] = state


def states_kernel(ks, extra, me_ref, q_hbm, k_hbm, v_hbm, d_hbm, *refs):
    held_ref, sems = refs[-2:]
    pairs = (k_hbm, v_hbm, q_hbm, d_hbm)
    every = ks + extra

    def copy(n, i):
        target = held_ref.at[n, i] if n < len(ks) else refs[2 * len(ks)].at[n - len(ks), i]
        return pltpu.make_async_copy(pairs[i].at[:, head_columns(me_ref, every[n])], target, sems.at[n, i])

    copies = [[copy(n, i) for i in range(4)] for n in range(len(every))]
    for group in copies:
        for item in group:
            item.start()
    for axis in range(2):
        for n in range(len(ks)):
            copies[n][2 * axis].wait()
            copies[n][2 * axis + 1].wait()
            sub_states(held_ref[n, 2 * axis], held_ref[n, 2 * axis + 1], axis, refs[2 * n + 1], refs[2 * n])
    for group in copies[len(ks) :]:
        for item in group:
            item.wait()


def state_shapes(length):
    return [
        jax.ShapeDtypeStruct((2, DH, DH), F32),
        jax.ShapeDtypeStruct((length // CHUNK, 2, DH, DH), F32),
    ]


def head_states(ks, extra, me, arrays):
    length = arrays[0].shape[0]
    every = len(ks) + len(extra)
    held = [jax.ShapeDtypeStruct((len(extra), 4, length, DH), BF16)] if extra else []
    return pl.pallas_call(
        functools.partial(states_kernel, ks, extra),
        out_shape=state_shapes(length) * len(ks) + held,
        in_specs=[SMEM] + [HBM] * 4,
        out_specs=[VMEM] * (2 * len(ks) + len(held)),
        scratch_shapes=[pltpu.VMEM((len(ks), 4, length, DH), BF16), pltpu.SemaphoreType.DMA((every, 4))],
        compiler_params=params(16),
        cost_estimate=pl.CostEstimate(
            flops=4 * len(ks) * length * DH * DH, bytes_accessed=8 * every * length * DH, transcendentals=0
        ),
        name="head_states",
    )(me, *arrays)


def held_kernel(held_ref, *refs):
    for n in range(held_ref.shape[0]):
        for axis in range(2):
            sub_states(held_ref[n, 2 * axis], held_ref[n, 2 * axis + 1], axis, refs[2 * n + 1], refs[2 * n])


def held_states(held):
    count, _, length, _ = held.shape
    return pl.pallas_call(
        held_kernel,
        out_shape=state_shapes(length) * count,
        in_specs=[VMEM],
        out_specs=[VMEM] * (2 * count),
        compiler_params=params(8),
        cost_estimate=pl.CostEstimate(
            flops=4 * count * length * DH * DH, bytes_accessed=8 * count * length * DH, transcendentals=0
        ),
        name="held_states",
    )(held)


def local_kernel(ks, me_ref, after_ref, q_ref, k_ref, v_ref, d_ref, *refs):
    length = q_ref.shape[0]
    rows = lax.broadcasted_iota(jnp.int32, (CHUNK, CHUNK), 0)
    cols = lax.broadcasted_iota(jnp.int32, (CHUNK, CHUNK), 1)
    lower = rows >= cols
    upper = rows <= cols
    for n, which in enumerate(ks):
        att_ref, gq_ref, gk_ref, gv_ref = refs[4 * n : 4 * n + 4]
        columns = head_columns(me_ref, which)
        for c in range(length // CHUNK):
            at = slice(c * CHUNK, (c + 1) * CHUNK)
            q, k, v, d = q_ref[at, columns], k_ref[at, columns], v_ref[at, columns], d_ref[at, columns]
            weights = jnp.where(lower, mm_last(q, k), 0.0).astype(BF16)
            back = jnp.where(lower, mm_last(d, v), 0.0).astype(BF16)
            weights_t = jnp.where(upper, mm_last(k, q), 0.0).astype(BF16)
            back_t = jnp.where(upper, mm_last(v, d), 0.0).astype(BF16)
            att_ref[at, :] = mm(weights, v)
            gq_ref[at, :] = mm(back, k)
            gk_ref[at, :] = mm(back_t, q)
            gv_ref[at, :] = mm(weights_t, d)
        if which == 0:
            total_ref, sub_ref = refs[-3:-1]
            sub_states(k_ref[:, columns], v_ref[:, columns], 0, sub_ref, total_ref)
            sub_states(q_ref[:, columns], d_ref[:, columns], 1, sub_ref, total_ref)
    refs[-1][...] = jnp.zeros_like(refs[-1])


def local_products(ks, me, arrays, after):
    length = arrays[0].shape[0]
    states = state_shapes(length) if 0 in ks else []
    results = pl.pallas_call(
        functools.partial(local_kernel, ks),
        out_shape=[jax.ShapeDtypeStruct((length, DH), F32)] * (4 * len(ks))
        + states
        + [jax.ShapeDtypeStruct((8, DH), F32)],
        in_specs=[SMEM] + [VMEM] * 5,
        out_specs=[VMEM] * (4 * len(ks) + len(states) + 1),
        compiler_params=params(16),
        cost_estimate=pl.CostEstimate(
            flops=16 * len(ks) * length * CHUNK * DH, bytes_accessed=8 * len(ks) * length * DH, transcendentals=0
        ),
        name="local_products",
    )(me, after, *arrays)
    return [results[4 * n : 4 * n + 4] for n in range(len(ks))], results[4 * len(ks) : -1], results[-1]


def final_kernel(factor, which, count, earlier, last, me_ref, q_ref, k_ref, v_ref, d_ref, *refs):
    given, refs = refs[:count], refs[count:]
    (att_ref, gq_ref, gk_ref, gv_ref, sub_ref), refs = refs[:5], refs[5:]
    staged, refs = refs[: len(earlier)], refs[len(earlier) :]
    columns = head_columns(me_ref, which)
    copies = []
    if last is None:
        (stage,) = refs
    else:
        *outs, stage, sems = refs[-6:]
    for row, (k, source) in enumerate(zip(earlier, staged)):
        for i in range(4):
            copies.append(pltpu.make_async_copy(source.at[i], outs[i].at[:, head_columns(me_ref, k)], sems.at[row, i]))
    for copy in copies:
        copy.start()
    chunks = q_ref.shape[0] // CHUNK
    prefix, suffix = given[0][0], given[0][1]
    if count == 2 and given[1].shape[0] == 1:
        high = lax.rem(lax.div(me_ref[0], QUAD), 2) == 1
        zero = jnp.zeros((DH, DH), F32)
        prefix += jnp.where(high, given[1][0], zero)
        suffix += jnp.where(high, zero, given[1][0])
    elif count == 2:
        prefix += given[1][0]
        suffix += given[1][1]
    states = [split(prefix + sub_ref[c, 0]) for c in range(chunks)]
    grads = [split(suffix + sub_ref[c, 1]) for c in range(chunks)]
    work = (
        (q_ref, states, mm, att_ref),
        (d_ref, states, mm_last, gq_ref),
        (v_ref, grads, mm_last, gk_ref),
        (k_ref, grads, mm, gv_ref),
    )
    for i, (source, parts, product, local) in enumerate(work):
        for c, (hi, lo) in enumerate(parts):
            at = slice(c * CHUNK, (c + 1) * CHUNK)
            rows = source[at, columns]
            value = local[at, :] + product(rows, hi) + product(rows, lo)
            stage[i, at, :] = (factor * value).astype(BF16)
        if last is not None:
            copy = pltpu.make_async_copy(stage.at[i], outs[i].at[:, columns], sems.at[len(earlier), i])
            copy.start()
            copies.append(copy)
    for copy in copies:
        copy.wait()


def head_outputs(factor, which, me, arrays, given, local, staged=(), outs=None):
    length, columns = arrays[0].shape
    staging = (4, length, DH)
    earlier = tuple(k for k, _ in staged)
    inputs = [me, *arrays, *given, *local, *(value for _, value in staged)]
    in_specs = [SMEM] + [VMEM] * (len(inputs) - 1)
    if outs is None:
        out_shape, out_specs = [jax.ShapeDtypeStruct(staging, BF16)], [VMEM]
        scratch, aliases = [], {}
    else:
        out_shape, out_specs = [jax.ShapeDtypeStruct((length, columns), BF16)] * 4, [HBM] * 4
        scratch = [pltpu.VMEM(staging, BF16), pltpu.SemaphoreType.DMA((len(earlier) + 1, 4))]
        aliases = {len(inputs) + i: i for i in range(len(outs))}
        in_specs += [HBM] * len(outs)
    return pl.pallas_call(
        functools.partial(final_kernel, factor, which, len(given), earlier, None if outs is None else bool(outs)),
        out_shape=out_shape,
        in_specs=in_specs,
        out_specs=out_specs,
        scratch_shapes=scratch,
        input_output_aliases=aliases,
        compiler_params=params(16),
        cost_estimate=pl.CostEstimate(
            flops=16 * length * DH * DH, bytes_accessed=8 * length * DH, transcendentals=0
        ),
        name="head_outputs",
    )(*inputs, *(outs or ()))


def total_kernel(me_ref, after_ref, *refs):
    pieces, out_ref = refs[:-1], refs[-1]
    total = pieces[0][...]
    for piece in pieces[1:]:
        total += piece[...]
    out_ref[...] = total


def part_kernel(bit, me_ref, after_ref, *refs):
    pieces, out_ref = refs[:-1], refs[-1]
    at = pl.ds(lax.rem(lax.div(me_ref[0], bit), 2), 1)
    total = pieces[0][at]
    for piece in pieces[1:]:
        total += piece[at]
    out_ref[...] = total


def combine(kernel, states, me, after, pieces, name):
    return pl.pallas_call(
        kernel,
        out_shape=jax.ShapeDtypeStruct((states, DH, DH), F32),
        in_specs=[SMEM] + [VMEM] * (1 + len(pieces)),
        out_specs=VMEM,
        compiler_params=params(4),
        name=name,
    )(me, after, *pieces)


def parts_kernel(me_ref, after_ref, *refs):
    pieces, outs = refs[:QUAD], refs[QUAD:]
    rank = lax.rem(me_ref[0], QUAD)
    zero = jnp.zeros((DH, DH), F32)
    for k, out in enumerate(outs):
        prefix, suffix = zero, zero
        for j, piece in enumerate(pieces):
            if j != k:
                before = (rank ^ j) < (rank ^ k)
                prefix += jnp.where(before, piece[0], zero)
                suffix += jnp.where(before, zero, piece[1])
        out[0] = prefix
        out[1] = suffix


def quad_parts(me, after, pieces):
    return pl.pallas_call(
        parts_kernel,
        out_shape=[jax.ShapeDtypeStruct((2, DH, DH), F32)] * QUAD,
        in_specs=[SMEM] + [VMEM] * (1 + QUAD),
        out_specs=[VMEM] * QUAD,
        compiler_params=params(4),
        name="quad_parts",
    )(me, after, *pieces)


def base_kernel(bits, me_ref, last_ref, *refs):
    parts, out_ref = refs[:-1], refs[-1]
    high = [lax.rem(lax.div(me_ref[0], bit), 2) == 1 for bit in bits]
    zero = jnp.zeros((DH, DH), F32)
    prefix = jnp.where(high[-1], last_ref[0], zero)
    suffix = jnp.where(high[-1], zero, last_ref[0])
    for up, part in zip(high, parts):
        prefix += jnp.where(up, part[0], zero)
        suffix += jnp.where(up, zero, part[1])
    out_ref[0] = prefix
    out_ref[1] = suffix


def quad_base(bits, me, last, parts):
    return pl.pallas_call(
        functools.partial(base_kernel, bits),
        out_shape=jax.ShapeDtypeStruct((2, DH, DH), F32),
        in_specs=[SMEM] + [VMEM] * (1 + len(parts)),
        out_specs=VMEM,
        compiler_params=params(4),
        name="quad_base",
    )(me, last, *parts)


def whole_kernel(me_ref, after_ref, base_ref, *refs):
    half = len(refs) // 2
    for part_ref, out_ref in zip(refs[:half], refs[half:]):
        if base_ref.shape[0] == 1:
            high = lax.rem(lax.div(me_ref[0], QUAD), 2) == 1
            zero = jnp.zeros((DH, DH), F32)
            out_ref[0] = part_ref[0] + jnp.where(high, base_ref[0], zero)
            out_ref[1] = part_ref[1] + jnp.where(high, zero, base_ref[0])
        else:
            out_ref[...] = part_ref[...] + base_ref[...]


def whole_states(me, after, base, parts):
    return pl.pallas_call(
        whole_kernel,
        out_shape=[jax.ShapeDtypeStruct((2, DH, DH), F32)] * len(parts),
        in_specs=[SMEM] + [VMEM] * (2 + len(parts)),
        out_specs=[VMEM] * len(parts),
        compiler_params=params(4),
        name="whole_states",
    )(me, after, base, *parts)


def swap(value, bit):
    return lax.ppermute(value, "ctx", [(i, i ^ bit) for i in range(lax.axis_size("ctx"))])


def on_device(queries, key_vectors, value_rows, cotangent):
    devices = lax.axis_size("ctx")
    factor = 1.0 / math.sqrt(DH * queries.shape[0] * devices)
    arrays = (queries, key_vectors, value_rows, cotangent)
    held = tuple(pltpu.with_memory_space_constraint(array, pltpu.HBM) for array in arrays)
    me = jnp.reshape(lax.axis_index("ctx"), (1,))
    local = [None] * QUAD
    subs = [None] * QUAD
    send1, subs[1], send2, subs[2], held3 = head_states((1, 2), (3,), me, held)
    send3, subs[3] = held_states(held3)
    got3 = swap(send3, 3)
    got2 = swap(send2, 2)
    got1 = swap(send1, 1)
    (local[0], local[1],), (keep, subs[0]), after = local_products((0, 1), me, arrays, send3)
    (local[2],), _, after = local_products((2,), me, arrays, after)
    pieces = (keep, got1, got2, got3)
    known = pieces
    bits = []
    parts = []
    bit = QUAD
    while bit * 2 < devices:
        total = combine(total_kernel, 2, me, after, known, "sum_states")
        part = swap(total, bit)
        bits.append(bit)
        parts.append(part)
        known = (total, part)
        bit *= 2
    bits.append(bit)
    chosen = combine(functools.partial(part_kernel, bit), 1, me, after, known, "pick_state")
    base = swap(chosen, bit)
    mine = quad_parts(me, chosen, pieces)
    early = {k: swap(mine[k], k) for k in EARLY}
    (local[3],), _, after = local_products((3,), me, arrays, mine[0])
    if parts:
        base = quad_base(tuple(bits), me, base, parts)
    late = [k for k in range(1, QUAD) if k not in EARLY]
    given = {0: (mine[0], base)}
    if late:
        for k, whole in zip(late, whole_states(me, after, base, [mine[k] for k in late])):
            given[k] = (swap(whole, k),)
    for k in EARLY:
        given[k] = (early[k], swap(base, k))
    outs = head_outputs(factor, 0, me, arrays, given[0], [*local[0], subs[0]], outs=())
    staged = [(k, head_outputs(factor, k, me, arrays, given[k], [*local[k], subs[k]])[0]) for k in ORDER[:2]]
    k = ORDER[2]
    return tuple(head_outputs(factor, k, me, arrays, given[k], [*local[k], subs[k]], staged, outs))


def solution(mesh):
    spec = P(("grp", "ctx"), None)
    return jax.shard_map(
        on_device, mesh=mesh, in_specs=(spec,) * 4, out_specs=(spec,) * 4, check_vma=False
    )
```

```python
import functools
import math

import jax
import jax.numpy as jnp
from jax import lax
from jax.experimental import pallas as pl
from jax.experimental.pallas import tpu as pltpu
from jax.sharding import PartitionSpec as P

DH = 128
HEADS = 4
QUAD = 4
PARTNERS = (0, 3, 2, 1)
EARLY = ()
ORDER = (3, 1, 2)
CHUNK = 256
F32 = jnp.float32
BF16 = jnp.bfloat16
MIB = 2**20
VMEM = pl.BlockSpec(memory_space=pltpu.VMEM)
SMEM = pl.BlockSpec(memory_space=pltpu.SMEM)
HBM = pl.BlockSpec(memory_space=pltpu.HBM)


def mm(left, right):
    return lax.dot_general(left, right, (((1,), (0,)), ((), ())), preferred_element_type=F32)


def mm_first(left, right):
    return lax.dot_general(left, right, (((0,), (0,)), ((), ())), preferred_element_type=F32)


def mm_last(left, right):
    return lax.dot_general(left, right, (((1,), (1,)), ((), ())), preferred_element_type=F32)


def split(state):
    hi = state.astype(BF16)
    return hi, (state - hi.astype(F32)).astype(BF16)


def head_columns(me_ref, k):
    return pl.ds(pl.multiple_of((lax.rem(me_ref[0], QUAD) ^ PARTNERS[k]) * DH, DH), DH)


def params(mib):
    return pltpu.CompilerParams(vmem_limit_bytes=mib * MIB)


def sub_states(left, right, axis, sub_ref, total_ref):
    chunks = left.shape[0] // CHUNK
    state = jnp.zeros((DH, DH), F32)
    for c in range(chunks) if axis == 0 else reversed(range(chunks)):
        at = slice(c * CHUNK, (c + 1) * CHUNK)
        sub_ref[c, axis] = state
        state = state + mm_first(left[at], right[at])
    total_ref[axis] = state


def states_kernel(ks, extra, me_ref, q_hbm, k_hbm, v_hbm, d_hbm, *refs):
    held_ref, sems = refs[-2:]
    pairs = (k_hbm, v_hbm, q_hbm, d_hbm)
    every = ks + extra

    def copy(n, i):
        target = held_ref.at[n, i] if n < len(ks) else refs[2 * len(ks)].at[n - len(ks), i]
        return pltpu.make_async_copy(pairs[i].at[:, head_columns(me_ref, every[n])], target, sems.at[n, i])

    copies = [[copy(n, i) for i in range(4)] for n in range(len(every))]
    for group in copies:
        for item in group:
            item.start()
    for axis in range(2):
        for n in range(len(ks)):
            copies[n][2 * axis].wait()
            copies[n][2 * axis + 1].wait()
            sub_states(held_ref[n, 2 * axis], held_ref[n, 2 * axis + 1], axis, refs[2 * n + 1], refs[2 * n])
    for group in copies[len(ks) :]:
        for item in group:
            item.wait()


def state_shapes(length):
    return [
        jax.ShapeDtypeStruct((2, DH, DH), F32),
        jax.ShapeDtypeStruct((length // CHUNK, 2, DH, DH), F32),
    ]


def head_states(ks, extra, me, arrays):
    length = arrays[0].shape[0]
    every = len(ks) + len(extra)
    held = [jax.ShapeDtypeStruct((len(extra), 4, length, DH), BF16)] if extra else []
    return pl.pallas_call(
        functools.partial(states_kernel, ks, extra),
        out_shape=state_shapes(length) * len(ks) + held,
        in_specs=[SMEM] + [HBM] * 4,
        out_specs=[VMEM] * (2 * len(ks) + len(held)),
        scratch_shapes=[pltpu.VMEM((len(ks), 4, length, DH), BF16), pltpu.SemaphoreType.DMA((every, 4))],
        compiler_params=params(16),
        cost_estimate=pl.CostEstimate(
            flops=4 * len(ks) * length * DH * DH, bytes_accessed=8 * every * length * DH, transcendentals=0
        ),
        name="head_states",
    )(me, *arrays)


def held_kernel(held_ref, *refs):
    for n in range(held_ref.shape[0]):
        for axis in range(2):
            sub_states(held_ref[n, 2 * axis], held_ref[n, 2 * axis + 1], axis, refs[2 * n + 1], refs[2 * n])


def held_states(held):
    count, _, length, _ = held.shape
    return pl.pallas_call(
        held_kernel,
        out_shape=state_shapes(length) * count,
        in_specs=[VMEM],
        out_specs=[VMEM] * (2 * count),
        compiler_params=params(8),
        cost_estimate=pl.CostEstimate(
            flops=4 * count * length * DH * DH, bytes_accessed=8 * count * length * DH, transcendentals=0
        ),
        name="held_states",
    )(held)


def local_kernel(ks, me_ref, after_ref, q_ref, k_ref, v_ref, d_ref, *refs):
    length = q_ref.shape[0]
    rows = lax.broadcasted_iota(jnp.int32, (CHUNK, CHUNK), 0)
    cols = lax.broadcasted_iota(jnp.int32, (CHUNK, CHUNK), 1)
    lower = rows >= cols
    upper = rows <= cols
    for n, which in enumerate(ks):
        att_ref, gq_ref, gk_ref, gv_ref = refs[4 * n : 4 * n + 4]
        columns = head_columns(me_ref, which)
        for c in range(length // CHUNK):
            at = slice(c * CHUNK, (c + 1) * CHUNK)
            q, k, v, d = q_ref[at, columns], k_ref[at, columns], v_ref[at, columns], d_ref[at, columns]
            weights = jnp.where(lower, mm_last(q, k), 0.0).astype(BF16)
            back = jnp.where(lower, mm_last(d, v), 0.0).astype(BF16)
            weights_t = jnp.where(upper, mm_last(k, q), 0.0).astype(BF16)
            back_t = jnp.where(upper, mm_last(v, d), 0.0).astype(BF16)
            att_ref[at, :] = mm(weights, v)
            gq_ref[at, :] = mm(back, k)
            gk_ref[at, :] = mm(back_t, q)
            gv_ref[at, :] = mm(weights_t, d)
        if which == 0:
            total_ref, sub_ref = refs[-3:-1]
            sub_states(k_ref[:, columns], v_ref[:, columns], 0, sub_ref, total_ref)
            sub_states(q_ref[:, columns], d_ref[:, columns], 1, sub_ref, total_ref)
    refs[-1][...] = jnp.zeros_like(refs[-1])


def local_products(ks, me, arrays, after):
    length = arrays[0].shape[0]
    states = state_shapes(length) if 0 in ks else []
    results = pl.pallas_call(
        functools.partial(local_kernel, ks),
        out_shape=[jax.ShapeDtypeStruct((length, DH), F32)] * (4 * len(ks))
        + states
        + [jax.ShapeDtypeStruct((8, DH), F32)],
        in_specs=[SMEM] + [VMEM] * 5,
        out_specs=[VMEM] * (4 * len(ks) + len(states) + 1),
        compiler_params=params(16),
        cost_estimate=pl.CostEstimate(
            flops=16 * len(ks) * length * CHUNK * DH, bytes_accessed=8 * len(ks) * length * DH, transcendentals=0
        ),
        name="local_products",
    )(me, after, *arrays)
    return [results[4 * n : 4 * n + 4] for n in range(len(ks))], results[4 * len(ks) : -1], results[-1]


def final_kernel(factor, which, count, earlier, last, me_ref, q_ref, k_ref, v_ref, d_ref, *refs):
    given, refs = refs[:count], refs[count:]
    (att_ref, gq_ref, gk_ref, gv_ref, sub_ref), refs = refs[:5], refs[5:]
    staged, refs = refs[: len(earlier)], refs[len(earlier) :]
    columns = head_columns(me_ref, which)
    copies = []
    if last is None:
        (stage,) = refs
    else:
        *outs, stage, sems = refs[-6:]
    for row, (k, source) in enumerate(zip(earlier, staged)):
        for i in range(4):
            copies.append(pltpu.make_async_copy(source.at[i], outs[i].at[:, head_columns(me_ref, k)], sems.at[row, i]))
    for copy in copies:
        copy.start()
    chunks = q_ref.shape[0] // CHUNK
    prefix, suffix = given[0][0], given[0][1]
    if count == 2 and given[1].shape[0] == 1:
        high = lax.rem(lax.div(me_ref[0], QUAD), 2) == 1
        zero = jnp.zeros((DH, DH), F32)
        prefix += jnp.where(high, given[1][0], zero)
        suffix += jnp.where(high, zero, given[1][0])
    elif count == 2:
        prefix += given[1][0]
        suffix += given[1][1]
    states = [split(prefix + sub_ref[c, 0]) for c in range(chunks)]
    grads = [split(suffix + sub_ref[c, 1]) for c in range(chunks)]
    work = (
        (q_ref, states, mm, att_ref),
        (d_ref, states, mm_last, gq_ref),
        (v_ref, grads, mm_last, gk_ref),
        (k_ref, grads, mm, gv_ref),
    )
    for i, (source, parts, product, local) in enumerate(work):
        for c, (hi, lo) in enumerate(parts):
            at = slice(c * CHUNK, (c + 1) * CHUNK)
            rows = source[at, columns]
            value = local[at, :] + product(rows, hi) + product(rows, lo)
            stage[i, at, :] = (factor * value).astype(BF16)
        if last is not None:
            copy = pltpu.make_async_copy(stage.at[i], outs[i].at[:, columns], sems.at[len(earlier), i])
            copy.start()
            copies.append(copy)
    for copy in copies:
        copy.wait()


def head_outputs(factor, which, me, arrays, given, local, staged=(), outs=None):
    length, columns = arrays[0].shape
    staging = (4, length, DH)
    earlier = tuple(k for k, _ in staged)
    inputs = [me, *arrays, *given, *local, *(value for _, value in staged)]
    in_specs = [SMEM] + [VMEM] * (len(inputs) - 1)
    if outs is None:
        out_shape, out_specs = [jax.ShapeDtypeStruct(staging, BF16)], [VMEM]
        scratch, aliases = [], {}
    else:
        out_shape, out_specs = [jax.ShapeDtypeStruct((length, columns), BF16)] * 4, [HBM] * 4
        scratch = [pltpu.VMEM(staging, BF16), pltpu.SemaphoreType.DMA((len(earlier) + 1, 4))]
        aliases = {len(inputs) + i: i for i in range(len(outs))}
        in_specs += [HBM] * len(outs)
    return pl.pallas_call(
        functools.partial(final_kernel, factor, which, len(given), earlier, None if outs is None else bool(outs)),
        out_shape=out_shape,
        in_specs=in_specs,
        out_specs=out_specs,
        scratch_shapes=scratch,
        input_output_aliases=aliases,
        compiler_params=params(16),
        cost_estimate=pl.CostEstimate(
            flops=16 * length * DH * DH, bytes_accessed=8 * length * DH, transcendentals=0
        ),
        name="head_outputs",
    )(*inputs, *(outs or ()))


def total_kernel(me_ref, after_ref, *refs):
    pieces, out_ref = refs[:-1], refs[-1]
    total = pieces[0][...]
    for piece in pieces[1:]:
        total += piece[...]
    out_ref[...] = total


def part_kernel(bit, me_ref, after_ref, *refs):
    pieces, out_ref = refs[:-1], refs[-1]
    at = pl.ds(lax.rem(lax.div(me_ref[0], bit), 2), 1)
    total = pieces[0][at]
    for piece in pieces[1:]:
        total += piece[at]
    out_ref[...] = total


def combine(kernel, states, me, after, pieces, name):
    return pl.pallas_call(
        kernel,
        out_shape=jax.ShapeDtypeStruct((states, DH, DH), F32),
        in_specs=[SMEM] + [VMEM] * (1 + len(pieces)),
        out_specs=VMEM,
        compiler_params=params(4),
        name=name,
    )(me, after, *pieces)


def parts_kernel(me_ref, after_ref, *refs):
    pieces, outs = refs[:QUAD], refs[QUAD:]
    rank = lax.rem(me_ref[0], QUAD)
    zero = jnp.zeros((DH, DH), F32)
    for k, out in enumerate(outs):
        prefix, suffix = zero, zero
        for j, piece in enumerate(pieces):
            if j != k:
                before = (rank ^ PARTNERS[j]) < (rank ^ PARTNERS[k])
                prefix += jnp.where(before, piece[0], zero)
                suffix += jnp.where(before, zero, piece[1])
        out[0] = prefix
        out[1] = suffix


def quad_parts(me, after, pieces):
    return pl.pallas_call(
        parts_kernel,
        out_shape=[jax.ShapeDtypeStruct((2, DH, DH), F32)] * QUAD,
        in_specs=[SMEM] + [VMEM] * (1 + QUAD),
        out_specs=[VMEM] * QUAD,
        compiler_params=params(4),
        name="quad_parts",
    )(me, after, *pieces)


def base_kernel(bits, me_ref, last_ref, *refs):
    parts, out_ref = refs[:-1], refs[-1]
    high = [lax.rem(lax.div(me_ref[0], bit), 2) == 1 for bit in bits]
    zero = jnp.zeros((DH, DH), F32)
    prefix = jnp.where(high[-1], last_ref[0], zero)
    suffix = jnp.where(high[-1], zero, last_ref[0])
    for up, part in zip(high, parts):
        prefix += jnp.where(up, part[0], zero)
        suffix += jnp.where(up, zero, part[1])
    out_ref[0] = prefix
    out_ref[1] = suffix


def quad_base(bits, me, last, parts):
    return pl.pallas_call(
        functools.partial(base_kernel, bits),
        out_shape=jax.ShapeDtypeStruct((2, DH, DH), F32),
        in_specs=[SMEM] + [VMEM] * (1 + len(parts)),
        out_specs=VMEM,
        compiler_params=params(4),
        name="quad_base",
    )(me, last, *parts)


def whole_kernel(me_ref, after_ref, base_ref, *refs):
    half = len(refs) // 2
    for part_ref, out_ref in zip(refs[:half], refs[half:]):
        if base_ref.shape[0] == 1:
            high = lax.rem(lax.div(me_ref[0], QUAD), 2) == 1
            zero = jnp.zeros((DH, DH), F32)
            out_ref[0] = part_ref[0] + jnp.where(high, base_ref[0], zero)
            out_ref[1] = part_ref[1] + jnp.where(high, zero, base_ref[0])
        else:
            out_ref[...] = part_ref[...] + base_ref[...]


def whole_states(me, after, base, parts):
    return pl.pallas_call(
        whole_kernel,
        out_shape=[jax.ShapeDtypeStruct((2, DH, DH), F32)] * len(parts),
        in_specs=[SMEM] + [VMEM] * (2 + len(parts)),
        out_specs=[VMEM] * len(parts),
        compiler_params=params(4),
        name="whole_states",
    )(me, after, base, *parts)


def swap(value, bit):
    return lax.ppermute(value, "ctx", [(i, i ^ bit) for i in range(lax.axis_size("ctx"))])


def on_device(queries, key_vectors, value_rows, cotangent):
    devices = lax.axis_size("ctx")
    factor = 1.0 / math.sqrt(DH * queries.shape[0] * devices)
    arrays = (queries, key_vectors, value_rows, cotangent)
    held = tuple(pltpu.with_memory_space_constraint(array, pltpu.HBM) for array in arrays)
    me = jnp.reshape(lax.axis_index("ctx"), (1,))
    local = [None] * QUAD
    subs = [None] * QUAD
    send1, subs[1], send2, subs[2], held3 = head_states((1, 2), (3,), me, held)
    send3, subs[3] = held_states(held3)
    got3 = swap(send3, PARTNERS[3])
    got2 = swap(send2, PARTNERS[2])
    got1 = swap(send1, PARTNERS[1])
    (local[0], local[1],), (keep, subs[0]), after = local_products((0, 1), me, arrays, send3)
    (local[2],), _, after = local_products((2,), me, arrays, after)
    pieces = (keep, got1, got2, got3)
    known = pieces
    bits = []
    parts = []
    bit = QUAD
    while bit * 2 < devices:
        total = combine(total_kernel, 2, me, after, known, "sum_states")
        part = swap(total, bit)
        bits.append(bit)
        parts.append(part)
        known = (total, part)
        bit *= 2
    bits.append(bit)
    chosen = combine(functools.partial(part_kernel, bit), 1, me, after, known, "pick_state")
    base = swap(chosen, bit)
    mine = quad_parts(me, chosen, pieces)
    early = {k: swap(mine[k], PARTNERS[k]) for k in EARLY}
    (local[3],), _, after = local_products((3,), me, arrays, mine[0])
    if parts:
        base = quad_base(tuple(bits), me, base, parts)
    late = [k for k in range(1, QUAD) if k not in EARLY]
    given = {0: (mine[0], base)}
    if late:
        for k, whole in zip(late, whole_states(me, after, base, [mine[k] for k in late])):
            given[k] = (swap(whole, PARTNERS[k]),)
    for k in EARLY:
        given[k] = (early[k], swap(base, PARTNERS[k]))
    outs = head_outputs(factor, 0, me, arrays, given[0], [*local[0], subs[0]], outs=())
    staged = [(k, head_outputs(factor, k, me, arrays, given[k], [*local[k], subs[k]])[0]) for k in ORDER[:2]]
    k = ORDER[2]
    return tuple(head_outputs(factor, k, me, arrays, given[k], [*local[k], subs[k]], staged, outs))


def solution(mesh):
    spec = P(("grp", "ctx"), None)
    return jax.shard_map(
        on_device, mesh=mesh, in_specs=(spec,) * 4, out_specs=(spec,) * 4, check_vma=False
    )
```

```python
import functools
import math

import jax
import jax.numpy as jnp
from jax import lax
from jax.experimental import pallas as pl
from jax.experimental.pallas import tpu as pltpu
from jax.sharding import PartitionSpec as P

DH = 128
HEADS = 4
QUAD = 4
PARTNERS = (0, 3, 2, 1)
EARLY = ()
ORDER = (3, 1, 2)
CHUNK = 256
F32 = jnp.float32
BF16 = jnp.bfloat16
MIB = 2**20
VMEM = pl.BlockSpec(memory_space=pltpu.VMEM)
SMEM = pl.BlockSpec(memory_space=pltpu.SMEM)
HBM = pl.BlockSpec(memory_space=pltpu.HBM)


def mm(left, right):
    return lax.dot_general(left, right, (((1,), (0,)), ((), ())), preferred_element_type=F32)


def mm_first(left, right):
    return lax.dot_general(left, right, (((0,), (0,)), ((), ())), preferred_element_type=F32)


def mm_last(left, right):
    return lax.dot_general(left, right, (((1,), (1,)), ((), ())), preferred_element_type=F32)


def split(state):
    hi = state.astype(BF16)
    return hi, (state - hi.astype(F32)).astype(BF16)


def head_columns(me_ref, k):
    return pl.ds(pl.multiple_of((lax.rem(me_ref[0], QUAD) ^ PARTNERS[k]) * DH, DH), DH)


def params(mib):
    return pltpu.CompilerParams(vmem_limit_bytes=mib * MIB)


def sub_states(left, right, axis, sub_ref, total_ref):
    chunks = left.shape[0] // CHUNK
    state = jnp.zeros((DH, DH), F32)
    for c in range(chunks) if axis == 0 else reversed(range(chunks)):
        at = slice(c * CHUNK, (c + 1) * CHUNK)
        sub_ref[c, axis] = state
        state = state + mm_first(left[at], right[at])
    total_ref[axis] = state


def states_kernel(ks, extra, me_ref, q_hbm, k_hbm, v_hbm, d_hbm, *refs):
    held_ref, sems = refs[-2:]
    pairs = (k_hbm, v_hbm, q_hbm, d_hbm)
    every = ks + extra

    def copy(n, i):
        target = held_ref.at[n, i] if n < len(ks) else refs[2 * len(ks)].at[n - len(ks), i]
        return pltpu.make_async_copy(pairs[i].at[:, head_columns(me_ref, every[n])], target, sems.at[n, i])

    copies = [[copy(n, i) for i in range(4)] for n in range(len(every))]
    for axis in range(2):
        for group in copies[: len(ks)]:
            group[2 * axis].start()
            group[2 * axis + 1].start()
    for group in copies[len(ks) :]:
        for item in group:
            item.start()
    for axis in range(2):
        for n in range(len(ks)):
            copies[n][2 * axis].wait()
            copies[n][2 * axis + 1].wait()
            sub_states(held_ref[n, 2 * axis], held_ref[n, 2 * axis + 1], axis, refs[2 * n + 1], refs[2 * n])
    for group in copies[len(ks) :]:
        for item in group:
            item.wait()


def state_shapes(length):
    return [
        jax.ShapeDtypeStruct((2, DH, DH), F32),
        jax.ShapeDtypeStruct((length // CHUNK, 2, DH, DH), F32),
    ]


def head_states(ks, extra, me, arrays):
    length = arrays[0].shape[0]
    every = len(ks) + len(extra)
    held = [jax.ShapeDtypeStruct((len(extra), 4, length, DH), BF16)] if extra else []
    return pl.pallas_call(
        functools.partial(states_kernel, ks, extra),
        out_shape=state_shapes(length) * len(ks) + held,
        in_specs=[SMEM] + [HBM] * 4,
        out_specs=[VMEM] * (2 * len(ks) + len(held)),
        scratch_shapes=[pltpu.VMEM((len(ks), 4, length, DH), BF16), pltpu.SemaphoreType.DMA((every, 4))],
        compiler_params=params(16),
        cost_estimate=pl.CostEstimate(
            flops=4 * len(ks) * length * DH * DH, bytes_accessed=8 * every * length * DH, transcendentals=0
        ),
        name="head_states",
    )(me, *arrays)


def held_kernel(held_ref, *refs):
    for n in range(held_ref.shape[0]):
        for axis in range(2):
            sub_states(held_ref[n, 2 * axis], held_ref[n, 2 * axis + 1], axis, refs[2 * n + 1], refs[2 * n])


def held_states(held):
    count, _, length, _ = held.shape
    return pl.pallas_call(
        held_kernel,
        out_shape=state_shapes(length) * count,
        in_specs=[VMEM],
        out_specs=[VMEM] * (2 * count),
        compiler_params=params(8),
        cost_estimate=pl.CostEstimate(
            flops=4 * count * length * DH * DH, bytes_accessed=8 * count * length * DH, transcendentals=0
        ),
        name="held_states",
    )(held)


def local_kernel(ks, me_ref, after_ref, q_ref, k_ref, v_ref, d_ref, *refs):
    length = q_ref.shape[0]
    rows = lax.broadcasted_iota(jnp.int32, (CHUNK, CHUNK), 0)
    cols = lax.broadcasted_iota(jnp.int32, (CHUNK, CHUNK), 1)
    lower = rows >= cols
    upper = rows <= cols
    for n, which in enumerate(ks):
        att_ref, gq_ref, gk_ref, gv_ref = refs[4 * n : 4 * n + 4]
        columns = head_columns(me_ref, which)
        for c in range(length // CHUNK):
            at = slice(c * CHUNK, (c + 1) * CHUNK)
            q, k, v, d = q_ref[at, columns], k_ref[at, columns], v_ref[at, columns], d_ref[at, columns]
            weights = jnp.where(lower, mm_last(q, k), 0.0).astype(BF16)
            back = jnp.where(lower, mm_last(d, v), 0.0).astype(BF16)
            weights_t = jnp.where(upper, mm_last(k, q), 0.0).astype(BF16)
            back_t = jnp.where(upper, mm_last(v, d), 0.0).astype(BF16)
            att_ref[at, :] = mm(weights, v)
            gq_ref[at, :] = mm(back, k)
            gk_ref[at, :] = mm(back_t, q)
            gv_ref[at, :] = mm(weights_t, d)
        if which == 0:
            total_ref, sub_ref = refs[-3:-1]
            sub_states(k_ref[:, columns], v_ref[:, columns], 0, sub_ref, total_ref)
            sub_states(q_ref[:, columns], d_ref[:, columns], 1, sub_ref, total_ref)
    refs[-1][...] = jnp.zeros_like(refs[-1])


def local_products(ks, me, arrays, after):
    length = arrays[0].shape[0]
    states = state_shapes(length) if 0 in ks else []
    results = pl.pallas_call(
        functools.partial(local_kernel, ks),
        out_shape=[jax.ShapeDtypeStruct((length, DH), F32)] * (4 * len(ks))
        + states
        + [jax.ShapeDtypeStruct((8, DH), F32)],
        in_specs=[SMEM] + [VMEM] * 5,
        out_specs=[VMEM] * (4 * len(ks) + len(states) + 1),
        compiler_params=params(16),
        cost_estimate=pl.CostEstimate(
            flops=16 * len(ks) * length * CHUNK * DH, bytes_accessed=8 * len(ks) * length * DH, transcendentals=0
        ),
        name="local_products",
    )(me, after, *arrays)
    return [results[4 * n : 4 * n + 4] for n in range(len(ks))], results[4 * len(ks) : -1], results[-1]


def final_kernel(factor, which, count, earlier, last, me_ref, q_ref, k_ref, v_ref, d_ref, *refs):
    given, refs = refs[:count], refs[count:]
    (att_ref, gq_ref, gk_ref, gv_ref, sub_ref), refs = refs[:5], refs[5:]
    staged, refs = refs[: len(earlier)], refs[len(earlier) :]
    columns = head_columns(me_ref, which)
    copies = []
    if last is None:
        (stage,) = refs
    else:
        *outs, stage, sems = refs[-6:]
    for row, (k, source) in enumerate(zip(earlier, staged)):
        for i in range(4):
            copies.append(pltpu.make_async_copy(source.at[i], outs[i].at[:, head_columns(me_ref, k)], sems.at[row, i]))
    for copy in copies:
        copy.start()
    chunks = q_ref.shape[0] // CHUNK
    prefix, suffix = given[0][0], given[0][1]
    if count == 2 and given[1].shape[0] == 1:
        high = lax.rem(lax.div(me_ref[0], QUAD), 2) == 1
        zero = jnp.zeros((DH, DH), F32)
        prefix += jnp.where(high, given[1][0], zero)
        suffix += jnp.where(high, zero, given[1][0])
    elif count == 2:
        prefix += given[1][0]
        suffix += given[1][1]
    states = [split(prefix + sub_ref[c, 0]) for c in range(chunks)]
    grads = [split(suffix + sub_ref[c, 1]) for c in range(chunks)]
    work = (
        (q_ref, states, mm, att_ref),
        (d_ref, states, mm_last, gq_ref),
        (v_ref, grads, mm_last, gk_ref),
        (k_ref, grads, mm, gv_ref),
    )
    for i, (source, parts, product, local) in enumerate(work):
        for c, (hi, lo) in enumerate(parts):
            at = slice(c * CHUNK, (c + 1) * CHUNK)
            rows = source[at, columns]
            value = local[at, :] + product(rows, hi) + product(rows, lo)
            stage[i, at, :] = (factor * value).astype(BF16)
        if last is not None:
            copy = pltpu.make_async_copy(stage.at[i], outs[i].at[:, columns], sems.at[len(earlier), i])
            copy.start()
            copies.append(copy)
    for copy in copies:
        copy.wait()


def head_outputs(factor, which, me, arrays, given, local, staged=(), outs=None):
    length, columns = arrays[0].shape
    staging = (4, length, DH)
    earlier = tuple(k for k, _ in staged)
    inputs = [me, *arrays, *given, *local, *(value for _, value in staged)]
    in_specs = [SMEM] + [VMEM] * (len(inputs) - 1)
    if outs is None:
        out_shape, out_specs = [jax.ShapeDtypeStruct(staging, BF16)], [VMEM]
        scratch, aliases = [], {}
    else:
        out_shape, out_specs = [jax.ShapeDtypeStruct((length, columns), BF16)] * 4, [HBM] * 4
        scratch = [pltpu.VMEM(staging, BF16), pltpu.SemaphoreType.DMA((len(earlier) + 1, 4))]
        aliases = {len(inputs) + i: i for i in range(len(outs))}
        in_specs += [HBM] * len(outs)
    return pl.pallas_call(
        functools.partial(final_kernel, factor, which, len(given), earlier, None if outs is None else bool(outs)),
        out_shape=out_shape,
        in_specs=in_specs,
        out_specs=out_specs,
        scratch_shapes=scratch,
        input_output_aliases=aliases,
        compiler_params=params(16),
        cost_estimate=pl.CostEstimate(
            flops=16 * length * DH * DH, bytes_accessed=8 * length * DH, transcendentals=0
        ),
        name="head_outputs",
    )(*inputs, *(outs or ()))


def total_kernel(me_ref, after_ref, *refs):
    pieces, out_ref = refs[:-1], refs[-1]
    total = pieces[0][...]
    for piece in pieces[1:]:
        total += piece[...]
    out_ref[...] = total


def part_kernel(bit, me_ref, after_ref, *refs):
    pieces, out_ref = refs[:-1], refs[-1]
    at = pl.ds(lax.rem(lax.div(me_ref[0], bit), 2), 1)
    total = pieces[0][at]
    for piece in pieces[1:]:
        total += piece[at]
    out_ref[...] = total


def combine(kernel, states, me, after, pieces, name):
    return pl.pallas_call(
        kernel,
        out_shape=jax.ShapeDtypeStruct((states, DH, DH), F32),
        in_specs=[SMEM] + [VMEM] * (1 + len(pieces)),
        out_specs=VMEM,
        compiler_params=params(4),
        name=name,
    )(me, after, *pieces)


def parts_kernel(me_ref, after_ref, *refs):
    pieces, outs = refs[:QUAD], refs[QUAD:]
    rank = lax.rem(me_ref[0], QUAD)
    zero = jnp.zeros((DH, DH), F32)
    for k, out in enumerate(outs):
        prefix, suffix = zero, zero
        for j, piece in enumerate(pieces):
            if j != k:
                before = (rank ^ PARTNERS[j]) < (rank ^ PARTNERS[k])
                prefix += jnp.where(before, piece[0], zero)
                suffix += jnp.where(before, zero, piece[1])
        out[0] = prefix
        out[1] = suffix


def quad_parts(me, after, pieces):
    return pl.pallas_call(
        parts_kernel,
        out_shape=[jax.ShapeDtypeStruct((2, DH, DH), F32)] * QUAD,
        in_specs=[SMEM] + [VMEM] * (1 + QUAD),
        out_specs=[VMEM] * QUAD,
        compiler_params=params(4),
        name="quad_parts",
    )(me, after, *pieces)


def base_kernel(bits, me_ref, last_ref, *refs):
    parts, out_ref = refs[:-1], refs[-1]
    high = [lax.rem(lax.div(me_ref[0], bit), 2) == 1 for bit in bits]
    zero = jnp.zeros((DH, DH), F32)
    prefix = jnp.where(high[-1], last_ref[0], zero)
    suffix = jnp.where(high[-1], zero, last_ref[0])
    for up, part in zip(high, parts):
        prefix += jnp.where(up, part[0], zero)
        suffix += jnp.where(up, zero, part[1])
    out_ref[0] = prefix
    out_ref[1] = suffix


def quad_base(bits, me, last, parts):
    return pl.pallas_call(
        functools.partial(base_kernel, bits),
        out_shape=jax.ShapeDtypeStruct((2, DH, DH), F32),
        in_specs=[SMEM] + [VMEM] * (1 + len(parts)),
        out_specs=VMEM,
        compiler_params=params(4),
        name="quad_base",
    )(me, last, *parts)


def whole_kernel(me_ref, after_ref, base_ref, *refs):
    half = len(refs) // 2
    for part_ref, out_ref in zip(refs[:half], refs[half:]):
        if base_ref.shape[0] == 1:
            high = lax.rem(lax.div(me_ref[0], QUAD), 2) == 1
            zero = jnp.zeros((DH, DH), F32)
            out_ref[0] = part_ref[0] + jnp.where(high, base_ref[0], zero)
            out_ref[1] = part_ref[1] + jnp.where(high, zero, base_ref[0])
        else:
            out_ref[...] = part_ref[...] + base_ref[...]


def whole_states(me, after, base, parts):
    return pl.pallas_call(
        whole_kernel,
        out_shape=[jax.ShapeDtypeStruct((2, DH, DH), F32)] * len(parts),
        in_specs=[SMEM] + [VMEM] * (2 + len(parts)),
        out_specs=[VMEM] * len(parts),
        compiler_params=params(4),
        name="whole_states",
    )(me, after, base, *parts)


def swap(value, bit):
    return lax.ppermute(value, "ctx", [(i, i ^ bit) for i in range(lax.axis_size("ctx"))])


def on_device(queries, key_vectors, value_rows, cotangent):
    devices = lax.axis_size("ctx")
    factor = 1.0 / math.sqrt(DH * queries.shape[0] * devices)
    arrays = (queries, key_vectors, value_rows, cotangent)
    held = tuple(pltpu.with_memory_space_constraint(array, pltpu.HBM) for array in arrays)
    me = jnp.reshape(lax.axis_index("ctx"), (1,))
    local = [None] * QUAD
    subs = [None] * QUAD
    send1, subs[1], send2, subs[2], held3 = head_states((1, 2), (3,), me, held)
    send3, subs[3] = held_states(held3)
    got3 = swap(send3, PARTNERS[3])
    got2 = swap(send2, PARTNERS[2])
    got1 = swap(send1, PARTNERS[1])
    (local[0], local[1],), (keep, subs[0]), after = local_products((0, 1), me, arrays, send3)
    (local[2],), _, after = local_products((2,), me, arrays, after)
    pieces = (keep, got1, got2, got3)
    known = pieces
    bits = []
    parts = []
    bit = QUAD
    while bit * 2 < devices:
        total = combine(total_kernel, 2, me, after, known, "sum_states")
        part = swap(total, bit)
        bits.append(bit)
        parts.append(part)
        known = (total, part)
        bit *= 2
    bits.append(bit)
    chosen = combine(functools.partial(part_kernel, bit), 1, me, after, known, "pick_state")
    base = swap(chosen, bit)
    mine = quad_parts(me, chosen, pieces)
    early = {k: swap(mine[k], PARTNERS[k]) for k in EARLY}
    (local[3],), _, after = local_products((3,), me, arrays, mine[0])
    if parts:
        base = quad_base(tuple(bits), me, base, parts)
    late = [k for k in range(1, QUAD) if k not in EARLY]
    given = {0: (mine[0], base)}
    if late:
        for k, whole in zip(late, whole_states(me, after, base, [mine[k] for k in late])):
            given[k] = (swap(whole, PARTNERS[k]),)
    for k in EARLY:
        given[k] = (early[k], swap(base, PARTNERS[k]))
    outs = head_outputs(factor, 0, me, arrays, given[0], [*local[0], subs[0]], outs=())
    staged = [(k, head_outputs(factor, k, me, arrays, given[k], [*local[k], subs[k]])[0]) for k in ORDER[:2]]
    k = ORDER[2]
    return tuple(head_outputs(factor, k, me, arrays, given[k], [*local[k], subs[k]], staged, outs))


def solution(mesh):
    spec = P(("grp", "ctx"), None)
    return jax.shard_map(
        on_device, mesh=mesh, in_specs=(spec,) * 4, out_specs=(spec,) * 4, check_vma=False
    )
```

```python
import functools
import math

import jax
import jax.numpy as jnp
from jax import lax
from jax.experimental import pallas as pl
from jax.experimental.pallas import tpu as pltpu
from jax.sharding import PartitionSpec as P

DH = 128
HEADS = 4
QUAD = 4
PARTNERS = (0, 3, 2, 1)
EARLY = ()
ORDER = (3, 1, 2)
CHUNK = 256
F32 = jnp.float32
BF16 = jnp.bfloat16
MIB = 2**20
VMEM = pl.BlockSpec(memory_space=pltpu.VMEM)
SMEM = pl.BlockSpec(memory_space=pltpu.SMEM)
HBM = pl.BlockSpec(memory_space=pltpu.HBM)


def mm(left, right):
    return lax.dot_general(left, right, (((1,), (0,)), ((), ())), preferred_element_type=F32)


def mm_first(left, right):
    return lax.dot_general(left, right, (((0,), (0,)), ((), ())), preferred_element_type=F32)


def mm_last(left, right):
    return lax.dot_general(left, right, (((1,), (1,)), ((), ())), preferred_element_type=F32)


def split(state):
    hi = state.astype(BF16)
    return hi, (state - hi.astype(F32)).astype(BF16)


def head_columns(me_ref, k):
    return pl.ds(pl.multiple_of((lax.rem(me_ref[0], QUAD) ^ PARTNERS[k]) * DH, DH), DH)


def params(mib):
    return pltpu.CompilerParams(vmem_limit_bytes=mib * MIB)


def sub_states(left, right, axis, sub_ref, total_ref):
    chunks = left.shape[0] // CHUNK
    state = jnp.zeros((DH, DH), F32)
    for c in range(chunks) if axis == 0 else reversed(range(chunks)):
        at = slice(c * CHUNK, (c + 1) * CHUNK)
        sub_ref[c, axis] = state
        state = state + mm_first(left[at], right[at])
    total_ref[axis] = state


def states_kernel(ks, extra, me_ref, q_hbm, k_hbm, v_hbm, d_hbm, *refs):
    held_ref, sems = refs[-2:]
    pairs = (k_hbm, v_hbm, q_hbm, d_hbm)
    every = ks + extra

    def copy(n, i):
        target = held_ref.at[n, i] if n < len(ks) else refs[2 * len(ks)].at[n - len(ks), i]
        return pltpu.make_async_copy(pairs[i].at[:, head_columns(me_ref, every[n])], target, sems.at[n, i])

    copies = [[copy(n, i) for i in range(4)] for n in range(len(every))]
    for axis in range(2):
        for group in copies[: len(ks)]:
            group[2 * axis].start()
            group[2 * axis + 1].start()
    for group in copies[len(ks) :]:
        for item in group:
            item.start()
    for axis in range(2):
        for n in range(len(ks)):
            copies[n][2 * axis].wait()
            copies[n][2 * axis + 1].wait()
            sub_states(held_ref[n, 2 * axis], held_ref[n, 2 * axis + 1], axis, refs[2 * n + 1], refs[2 * n])
    for group in copies[len(ks) :]:
        for item in group:
            item.wait()


def state_shapes(length):
    return [
        jax.ShapeDtypeStruct((2, DH, DH), F32),
        jax.ShapeDtypeStruct((length // CHUNK, 2, DH, DH), F32),
    ]


def head_states(ks, extra, me, arrays):
    length = arrays[0].shape[0]
    every = len(ks) + len(extra)
    held = [jax.ShapeDtypeStruct((len(extra), 4, length, DH), BF16)] if extra else []
    return pl.pallas_call(
        functools.partial(states_kernel, ks, extra),
        out_shape=state_shapes(length) * len(ks) + held,
        in_specs=[SMEM] + [HBM] * 4,
        out_specs=[VMEM] * (2 * len(ks) + len(held)),
        scratch_shapes=[pltpu.VMEM((len(ks), 4, length, DH), BF16), pltpu.SemaphoreType.DMA((every, 4))],
        compiler_params=params(16),
        cost_estimate=pl.CostEstimate(
            flops=4 * len(ks) * length * DH * DH, bytes_accessed=8 * every * length * DH, transcendentals=0
        ),
        name="head_states",
    )(me, *arrays)


def held_kernel(held_ref, *refs):
    for n in range(held_ref.shape[0]):
        for axis in range(2):
            sub_states(held_ref[n, 2 * axis], held_ref[n, 2 * axis + 1], axis, refs[2 * n + 1], refs[2 * n])


def held_states(held):
    count, _, length, _ = held.shape
    return pl.pallas_call(
        held_kernel,
        out_shape=state_shapes(length) * count,
        in_specs=[VMEM],
        out_specs=[VMEM] * (2 * count),
        compiler_params=params(8),
        cost_estimate=pl.CostEstimate(
            flops=4 * count * length * DH * DH, bytes_accessed=8 * count * length * DH, transcendentals=0
        ),
        name="held_states",
    )(held)


def local_kernel(ks, me_ref, after_ref, q_ref, k_ref, v_ref, d_ref, *refs):
    length = q_ref.shape[0]
    rows = lax.broadcasted_iota(jnp.int32, (CHUNK, CHUNK), 0)
    cols = lax.broadcasted_iota(jnp.int32, (CHUNK, CHUNK), 1)
    lower = rows >= cols
    upper = rows <= cols
    for n, which in enumerate(ks):
        att_ref, gq_ref, gk_ref, gv_ref = refs[4 * n : 4 * n + 4]
        columns = head_columns(me_ref, which)
        for c in range(length // CHUNK):
            at = slice(c * CHUNK, (c + 1) * CHUNK)
            q, k, v, d = q_ref[at, columns], k_ref[at, columns], v_ref[at, columns], d_ref[at, columns]
            weights = jnp.where(lower, mm_last(q, k), 0.0).astype(BF16)
            back = jnp.where(lower, mm_last(d, v), 0.0).astype(BF16)
            weights_t = jnp.where(upper, mm_last(k, q), 0.0).astype(BF16)
            back_t = jnp.where(upper, mm_last(v, d), 0.0).astype(BF16)
            att_ref[at, :] = mm(weights, v)
            gq_ref[at, :] = mm(back, k)
            gk_ref[at, :] = mm(back_t, q)
            gv_ref[at, :] = mm(weights_t, d)
        if which == 0:
            total_ref, sub_ref = refs[-3:-1]
            sub_states(k_ref[:, columns], v_ref[:, columns], 0, sub_ref, total_ref)
            sub_states(q_ref[:, columns], d_ref[:, columns], 1, sub_ref, total_ref)
    refs[-1][...] = jnp.zeros_like(refs[-1])


def local_products(ks, me, arrays, after):
    length = arrays[0].shape[0]
    states = state_shapes(length) if 0 in ks else []
    results = pl.pallas_call(
        functools.partial(local_kernel, ks),
        out_shape=[jax.ShapeDtypeStruct((length, DH), F32)] * (4 * len(ks))
        + states
        + [jax.ShapeDtypeStruct((8, DH), F32)],
        in_specs=[SMEM] + [VMEM] * 5,
        out_specs=[VMEM] * (4 * len(ks) + len(states) + 1),
        compiler_params=params(16),
        cost_estimate=pl.CostEstimate(
            flops=16 * len(ks) * length * CHUNK * DH, bytes_accessed=8 * len(ks) * length * DH, transcendentals=0
        ),
        name="local_products",
    )(me, after, *arrays)
    return [results[4 * n : 4 * n + 4] for n in range(len(ks))], results[4 * len(ks) : -1], results[-1]


def final_kernel(factor, which, count, earlier, last, me_ref, q_ref, k_ref, v_ref, d_ref, *refs):
    given, refs = refs[:count], refs[count:]
    (att_ref, gq_ref, gk_ref, gv_ref, sub_ref), refs = refs[:5], refs[5:]
    staged, refs = refs[: len(earlier)], refs[len(earlier) :]
    columns = head_columns(me_ref, which)
    copies = []
    if last is None:
        (stage,) = refs
    else:
        *outs, stage, sems = refs[-6:]
    for row, (k, source) in enumerate(zip(earlier, staged)):
        for i in range(4):
            copies.append(pltpu.make_async_copy(source.at[i], outs[i].at[:, head_columns(me_ref, k)], sems.at[row, i]))
    for copy in copies:
        copy.start()
    chunks = q_ref.shape[0] // CHUNK
    prefix, suffix = given[0][0], given[0][1]
    if count == 2 and given[1].shape[0] == 1:
        high = lax.rem(lax.div(me_ref[0], QUAD), 2) == 1
        zero = jnp.zeros((DH, DH), F32)
        prefix += jnp.where(high, given[1][0], zero)
        suffix += jnp.where(high, zero, given[1][0])
    elif count == 2:
        prefix += given[1][0]
        suffix += given[1][1]
    states = [split(prefix + sub_ref[c, 0]) for c in range(chunks)]
    grads = [split(suffix + sub_ref[c, 1]) for c in range(chunks)]
    work = (
        (q_ref, states, mm, att_ref),
        (d_ref, states, mm_last, gq_ref),
        (v_ref, grads, mm_last, gk_ref),
        (k_ref, grads, mm, gv_ref),
    )
    for i, (source, parts, product, local) in enumerate(work):
        for c, (hi, lo) in enumerate(parts):
            at = slice(c * CHUNK, (c + 1) * CHUNK)
            rows = source[at, columns]
            value = local[at, :] + product(rows, hi) + product(rows, lo)
            stage[i, at, :] = (factor * value).astype(BF16)
            if last is not None and (c + 1) % (chunks // 2) == 0:
                half = (c + 1) // (chunks // 2) - 1
                part = slice(half * (chunks // 2) * CHUNK, (c + 1) * CHUNK)
                copy = pltpu.make_async_copy(
                    stage.at[i, part], outs[i].at[part, columns], sems.at[len(earlier) + half, i]
                )
                copy.start()
                copies.append(copy)
    for copy in copies:
        copy.wait()


def head_outputs(factor, which, me, arrays, given, local, staged=(), outs=None):
    length, columns = arrays[0].shape
    staging = (4, length, DH)
    earlier = tuple(k for k, _ in staged)
    inputs = [me, *arrays, *given, *local, *(value for _, value in staged)]
    in_specs = [SMEM] + [VMEM] * (len(inputs) - 1)
    if outs is None:
        out_shape, out_specs = [jax.ShapeDtypeStruct(staging, BF16)], [VMEM]
        scratch, aliases = [], {}
    else:
        out_shape, out_specs = [jax.ShapeDtypeStruct((length, columns), BF16)] * 4, [HBM] * 4
        scratch = [pltpu.VMEM(staging, BF16), pltpu.SemaphoreType.DMA((len(earlier) + 2, 4))]
        aliases = {len(inputs) + i: i for i in range(len(outs))}
        in_specs += [HBM] * len(outs)
    return pl.pallas_call(
        functools.partial(final_kernel, factor, which, len(given), earlier, None if outs is None else bool(outs)),
        out_shape=out_shape,
        in_specs=in_specs,
        out_specs=out_specs,
        scratch_shapes=scratch,
        input_output_aliases=aliases,
        compiler_params=params(16),
        cost_estimate=pl.CostEstimate(
            flops=16 * length * DH * DH, bytes_accessed=8 * length * DH, transcendentals=0
        ),
        name="head_outputs",
    )(*inputs, *(outs or ()))


def total_kernel(me_ref, after_ref, *refs):
    pieces, out_ref = refs[:-1], refs[-1]
    total = pieces[0][...]
    for piece in pieces[1:]:
        total += piece[...]
    out_ref[...] = total


def part_kernel(bit, me_ref, after_ref, *refs):
    pieces, out_ref = refs[:-1], refs[-1]
    at = pl.ds(lax.rem(lax.div(me_ref[0], bit), 2), 1)
    total = pieces[0][at]
    for piece in pieces[1:]:
        total += piece[at]
    out_ref[...] = total


def combine(kernel, states, me, after, pieces, name):
    return pl.pallas_call(
        kernel,
        out_shape=jax.ShapeDtypeStruct((states, DH, DH), F32),
        in_specs=[SMEM] + [VMEM] * (1 + len(pieces)),
        out_specs=VMEM,
        compiler_params=params(4),
        name=name,
    )(me, after, *pieces)


def parts_kernel(me_ref, after_ref, *refs):
    pieces, outs = refs[:QUAD], refs[QUAD:]
    rank = lax.rem(me_ref[0], QUAD)
    zero = jnp.zeros((DH, DH), F32)
    for k, out in enumerate(outs):
        prefix, suffix = zero, zero
        for j, piece in enumerate(pieces):
            if j != k:
                before = (rank ^ PARTNERS[j]) < (rank ^ PARTNERS[k])
                prefix += jnp.where(before, piece[0], zero)
                suffix += jnp.where(before, zero, piece[1])
        out[0] = prefix
        out[1] = suffix


def quad_parts(me, after, pieces):
    return pl.pallas_call(
        parts_kernel,
        out_shape=[jax.ShapeDtypeStruct((2, DH, DH), F32)] * QUAD,
        in_specs=[SMEM] + [VMEM] * (1 + QUAD),
        out_specs=[VMEM] * QUAD,
        compiler_params=params(4),
        name="quad_parts",
    )(me, after, *pieces)


def base_kernel(bits, me_ref, last_ref, *refs):
    parts, out_ref = refs[:-1], refs[-1]
    high = [lax.rem(lax.div(me_ref[0], bit), 2) == 1 for bit in bits]
    zero = jnp.zeros((DH, DH), F32)
    prefix = jnp.where(high[-1], last_ref[0], zero)
    suffix = jnp.where(high[-1], zero, last_ref[0])
    for up, part in zip(high, parts):
        prefix += jnp.where(up, part[0], zero)
        suffix += jnp.where(up, zero, part[1])
    out_ref[0] = prefix
    out_ref[1] = suffix


def quad_base(bits, me, last, parts):
    return pl.pallas_call(
        functools.partial(base_kernel, bits),
        out_shape=jax.ShapeDtypeStruct((2, DH, DH), F32),
        in_specs=[SMEM] + [VMEM] * (1 + len(parts)),
        out_specs=VMEM,
        compiler_params=params(4),
        name="quad_base",
    )(me, last, *parts)


def whole_kernel(me_ref, after_ref, base_ref, *refs):
    half = len(refs) // 2
    for part_ref, out_ref in zip(refs[:half], refs[half:]):
        if base_ref.shape[0] == 1:
            high = lax.rem(lax.div(me_ref[0], QUAD), 2) == 1
            zero = jnp.zeros((DH, DH), F32)
            out_ref[0] = part_ref[0] + jnp.where(high, base_ref[0], zero)
            out_ref[1] = part_ref[1] + jnp.where(high, zero, base_ref[0])
        else:
            out_ref[...] = part_ref[...] + base_ref[...]


def whole_states(me, after, base, parts):
    return pl.pallas_call(
        whole_kernel,
        out_shape=[jax.ShapeDtypeStruct((2, DH, DH), F32)] * len(parts),
        in_specs=[SMEM] + [VMEM] * (2 + len(parts)),
        out_specs=[VMEM] * len(parts),
        compiler_params=params(4),
        name="whole_states",
    )(me, after, base, *parts)


def swap(value, bit):
    return lax.ppermute(value, "ctx", [(i, i ^ bit) for i in range(lax.axis_size("ctx"))])


def on_device(queries, key_vectors, value_rows, cotangent):
    devices = lax.axis_size("ctx")
    factor = 1.0 / math.sqrt(DH * queries.shape[0] * devices)
    arrays = (queries, key_vectors, value_rows, cotangent)
    held = tuple(pltpu.with_memory_space_constraint(array, pltpu.HBM) for array in arrays)
    me = jnp.reshape(lax.axis_index("ctx"), (1,))
    local = [None] * QUAD
    subs = [None] * QUAD
    send1, subs[1], send2, subs[2], held3 = head_states((1, 2), (3,), me, held)
    send3, subs[3] = held_states(held3)
    got3 = swap(send3, PARTNERS[3])
    got2 = swap(send2, PARTNERS[2])
    got1 = swap(send1, PARTNERS[1])
    (local[0], local[1],), (keep, subs[0]), after = local_products((0, 1), me, arrays, send3)
    (local[2],), _, after = local_products((2,), me, arrays, after)
    pieces = (keep, got1, got2, got3)
    known = pieces
    bits = []
    parts = []
    bit = QUAD
    while bit * 2 < devices:
        total = combine(total_kernel, 2, me, after, known, "sum_states")
        part = swap(total, bit)
        bits.append(bit)
        parts.append(part)
        known = (total, part)
        bit *= 2
    bits.append(bit)
    chosen = combine(functools.partial(part_kernel, bit), 1, me, after, known, "pick_state")
    base = swap(chosen, bit)
    mine = quad_parts(me, chosen, pieces)
    early = {k: swap(mine[k], PARTNERS[k]) for k in EARLY}
    (local[3],), _, after = local_products((3,), me, arrays, mine[0])
    if parts:
        base = quad_base(tuple(bits), me, base, parts)
    late = [k for k in range(1, QUAD) if k not in EARLY]
    given = {0: (mine[0], base)}
    if late:
        for k, whole in zip(late, whole_states(me, after, base, [mine[k] for k in late])):
            given[k] = (swap(whole, PARTNERS[k]),)
    for k in EARLY:
        given[k] = (early[k], swap(base, PARTNERS[k]))
    outs = head_outputs(factor, 0, me, arrays, given[0], [*local[0], subs[0]], outs=())
    staged = [(k, head_outputs(factor, k, me, arrays, given[k], [*local[k], subs[k]])[0]) for k in ORDER[:2]]
    k = ORDER[2]
    return tuple(head_outputs(factor, k, me, arrays, given[k], [*local[k], subs[k]], staged, outs))


def solution(mesh):
    spec = P(("grp", "ctx"), None)
    return jax.shard_map(
        on_device, mesh=mesh, in_specs=(spec,) * 4, out_specs=(spec,) * 4, check_vma=False
    )
```
